32 devices in a mesh: src: 4 (over y, x), tgt: 8 (over z, core).
Axes of the slice: x: 2, y: 2, z: 4, core: 2. Of those that a mesh axis runs over, the one named last changes fastest.
Arguments:
- src_emb_t: bfloat16 [300, 4096], P(None, 'src'), may hold values from -6 to 6
- tgt_emb_t: bfloat16 [300, 16384], P(None, 'tgt'), may hold values from -6 to 6
- core: float32 [300, 300], replicated, may hold values from -0.08 to 0.2
- src_logw: float32 [4096], P('src'), may hold values from -1.5 to 1.5
- tgt_logw: float32 [16384], P('tgt'), may hold values from -1.5 to 1.5
Outputs:
- src_potential: float32 [4096], P('src')
- tgt_potential: float32 [16384], P('tgt')
- next_core: float32 [300, 300], replicated
The draws below stay inside these ranges and needn't reach their ends.
All inputs are finite; a program needn't handle non-finite values.
Results may differ from the reference program's by a relative error of at most 0.0036.
Values sent between devices are 32-bit elements; how exact they have to be, the bound alone decides.
A program may use at most 64 MiB of HBM per device.

```python
import jax
import jax.numpy as jnp
from jax import lax

D = 300
ROWS = 1024
ITERS = 3
NS = 4096
NT = 16384
N_SRC = 4


def embed_pair(key):
    base = jax.random.fold_in(key, 11)
    key_src = jax.random.fold_in(base, 0)
    key_tgt = jax.random.fold_in(base, 1)
    key_cols = jax.random.fold_in(base, 3)
    source = jnp.clip(1.0 + jax.random.normal(key_src, (D, NS), jnp.float32), -6.0, 6.0)
    target = jnp.clip(jax.random.normal(key_tgt, (D, NT), jnp.float32), -6.0, 6.0)
    shunned = jax.random.randint(key_cols, (4,), 0, NT - 8)
    column_index = jnp.arange(NT)[None, :]
    hit = jnp.any(column_index[:, :, None] == shunned[None, None, :], axis=2)
    target = jnp.where(hit, -6.0, target).astype(jnp.float32)
    return (source, target)


def draw_src_emb_t(key, part):
    source, target = embed_pair(key)
    return source.astype(jnp.bfloat16)


def draw_tgt_emb_t(key, part):
    source, target = embed_pair(key)
    return target.astype(jnp.bfloat16)


def draw_core(key, part):
    inner = jax.random.fold_in(key, 5)
    noise = jnp.clip(jax.random.normal(inner, (D, D), jnp.float32), -4.0, 4.0)
    return (noise + 6.0 * jnp.eye(D, dtype=jnp.float32)) * (6.0 / D)


def level_of(key, shape, cuts, smallest, top_value):
    def one(dim, shards_of):
        draws = jax.random.uniform(jax.random.fold_in(jax.random.fold_in(key, 6), dim), (shards_of,), jnp.float32, smallest / len(cuts), top_value / len(cuts))
        return jnp.repeat(jnp.exp(draws), shape[dim] // shards_of).reshape((-1,) + (1,) * (len(shape) - dim - 1))

    loudness = one(*cuts[0])
    for cut in cuts[1:]:
        loudness = loudness * one(*cut)
    return loudness


def setup_inputs(seed: int = 0) -> dict:
    streams_of = jax.random.split(jax.random.key(seed), 6)
    src_emb_t = draw_src_emb_t(jax.random.fold_in(streams_of[5], 71), 0)
    tgt_emb_t = draw_tgt_emb_t(jax.random.fold_in(streams_of[5], 71), 0)
    core = draw_core(jax.random.fold_in(streams_of[5], 71), 0)
    src_logw = jnp.clip(jax.random.uniform(streams_of[3], (NS,), jnp.float32, -1.5, 1.5) * level_of(streams_of[3], (NS,), ((0, 4),), -0.4, 0.0), -1.5, 1.5)
    tgt_logw = jnp.clip(jax.random.uniform(streams_of[4], (NT,), jnp.float32, -1.5, 1.5) * level_of(streams_of[4], (NT,), ((0, 8),), -0.4, 0.0), -1.5, 1.5)
    return dict(src_emb_t=src_emb_t, tgt_emb_t=tgt_emb_t, core=core, src_logw=src_logw, tgt_logw=tgt_logw)


def reference(src_emb_t, tgt_emb_t, core, src_logw, tgt_logw):
    projected = jnp.dot(core.T, src_emb_t.astype(jnp.float32), precision=lax.Precision.HIGHEST).astype(jnp.bfloat16)
    proj_blocks = projected.reshape(D, N_SRC, ROWS).transpose(1, 0, 2)
    emb_blocks = src_emb_t.reshape(D, N_SRC, ROWS).transpose(1, 0, 2)
    logw_blocks = src_logw.reshape(N_SRC, ROWS)

    def scores_of(block):
        return lax.dot_general(block, tgt_emb_t, (((0,), (0,)), ((), ())), preferred_element_type=jnp.float32)

    tgt_pot = jnp.zeros((NT,), jnp.float32)
    src_pot = jnp.zeros((NS,), jnp.float32)
    for step in range(ITERS):
        def row_step(inputs):
            block, logw = inputs
            shifted = scores_of(block) + tgt_pot[None, :]
            peaks = jnp.max(shifted, axis=1)
            totals = jnp.sum(jnp.exp(shifted - peaks[:, None]), axis=1)
            return logw - (peaks + jnp.log(totals))

        src_pot = lax.map(row_step, (proj_blocks, logw_blocks)).reshape(NS)
        pot_blocks = src_pot.reshape(N_SRC, ROWS)

        def col_step(carry, inputs):
            peaks, totals = carry
            block, pot = inputs
            shifted = scores_of(block) + pot[:, None]
            newpeak = jnp.maximum(peaks, jnp.max(shifted, axis=0))
            totals = totals * jnp.exp(peaks - newpeak) + jnp.sum(jnp.exp(shifted - newpeak[None, :]), axis=0)
            return (newpeak, totals), None

        start = (jnp.full((NT,), -1e30, jnp.float32), jnp.zeros((NT,), jnp.float32))
        (peaks, totals), unused = lax.scan(col_step, start, (proj_blocks, pot_blocks))
        tgt_pot = tgt_logw - (peaks + jnp.log(totals))

    pot_blocks = src_pot.reshape(N_SRC, ROWS)

    def core_step(acc, inputs):
        block, emb, pot = inputs
        plan = jnp.exp(scores_of(block) + pot[:, None] + tgt_pot[None, :]).astype(jnp.bfloat16)
        panel = lax.dot_general(plan, tgt_emb_t, (((1,), (1,)), ((), ())), preferred_element_type=jnp.float32)
        return acc + jnp.dot(emb.astype(jnp.float32), panel, precision=lax.Precision.HIGHEST), None

    acc, unused = lax.scan(core_step, jnp.zeros((D, D), jnp.float32), (proj_blocks, emb_blocks, pot_blocks))
    next_core = acc * (D / NS)
    return src_pot, tgt_pot, next_core
```

```python
import functools
import math

import jax
import jax.numpy as jnp
from jax import lax
from jax.experimental import pallas as pl
from jax.experimental.pallas import tpu as pltpu
from jax.sharding import PartitionSpec as P

ITERS = 3
LOG2E = 1.4426950408889634
LN2 = 0.6931471805599453
LANES = 128
SHIFT = 60.0
MESH = pl.DeviceIdType.MESH


def tile(t):
    return slice(t * LANES, (t + 1) * LANES)


def kernel(
    n_src, n_tgt,
    src_ref, tgt_ref, core_ref, slw_ref, tlw_ref,
    f_out, g_out, core_out,
    S, proj, M, T, FB, FS, GS, RXF, RXG, plan, CB, RX1, RX2, RX3, OUT,
    fsend, frecv, gsend, grecv, s1, r1, s2, r2, s3, r3, s4, r4, s5, r5, s6, r6,
):
    si, ti = lax.axis_index("src"), lax.axis_index("tgt")
    dim, rows = src_ref.shape
    cols = tgt_ref.shape[1]
    rc, cc = rows // LANES, cols // LANES
    f32, bf16 = jnp.float32, jnp.bfloat16

    def src_peers():
        return [lax.rem(si + k, n_src) for k in range(1, n_src)]

    def tgt_peers():
        return [lax.rem(ti + k, n_tgt) for k in range(1, n_tgt)]

    barrier = pltpu.get_barrier_semaphore()
    for p in src_peers():
        pl.semaphore_signal(barrier, inc=1, device_id=(p, ti), device_id_type=MESH)
    for p in tgt_peers():
        pl.semaphore_signal(barrier, inc=1, device_id=(si, p), device_id_type=MESH)

    c32 = core_ref[...]
    c0 = c32.astype(bf16)
    left = c32 - c0.astype(f32)
    c1 = left.astype(bf16)
    c2 = (left - c1.astype(f32)).astype(bf16)
    src = src_ref[...]

    def contract(a, b, da, db):
        return lax.dot_general(a, b, (((da,), (db,)), ((), ())), preferred_element_type=f32)

    proj[...] = (
        contract(src, c0, 0, 0) + (contract(src, c1, 0, 0) + contract(src, c2, 0, 0))
    ).astype(bf16)

    M[...] = jnp.full((rows, LANES), -jnp.inf, f32)
    wide = 2 * LANES

    def score_tile(t, carry):
        at = pl.ds(pl.multiple_of(t * wide, wide), wide)
        y = jnp.dot(proj[...], tgt_ref[:, at], preferred_element_type=f32) * LOG2E
        S[:, at] = y
        M[...] = jnp.maximum(M[...], jnp.maximum(y[:, :LANES], y[:, LANES:]))
        return carry

    lax.fori_loop(0, cols // wide, score_tile, 0)

    def groups(body, carry, unroll):
        def step(i, carry):
            for k in range(unroll):
                carry = body(pl.ds(pl.multiple_of((i * unroll + k) * 8, 8), 8), carry)
            return carry

        return lax.fori_loop(0, rows // (8 * unroll), step, carry)

    def first_rows(r, carry):
        m = M[r, :]
        parts = [jnp.exp2(S[r, tile(t)] - m) for t in range(cc)]
        while len(parts) > 1:
            parts = [a + b for a, b in zip(parts[::2], parts[1::2])]
        T[r, :] = parts[0]
        return carry

    groups(first_rows, 0, 4)

    def broadcast_down(line):
        return jnp.broadcast_to(line, (8, LANES))

    def to_columns(dense):
        for c in range(rc):
            FB[tile(c), :] = jnp.broadcast_to(dense[c : c + 1, :], (LANES, LANES)).T

    def exchange(buf, step, me, peers, send, recv, where):
        copies = []
        for k, p in enumerate(peers):
            copy = pltpu.make_async_remote_copy(
                src_ref=buf.at[step, me],
                dst_ref=buf.at[step, me],
                send_sem=send.at[step, k],
                recv_sem=recv.at[step, me],
                device_id=where(p),
                device_id_type=MESH,
            )
            copy.start()
            copies.append(copy)
        for k, p in enumerate(peers):
            pltpu.make_async_remote_copy(
                src_ref=buf.at[step, p],
                dst_ref=buf.at[step, p],
                send_sem=send.at[step, k],
                recv_sem=recv.at[step, p],
                device_id=where(p),
                device_id_type=MESH,
            ).wait_recv()
        return copies

    def share_rows(step):
        RXF[step, ti] = FS[...]
        return exchange(RXF, step, ti, tgt_peers(), fsend, frecv, lambda p: (si, p))

    def share_cols(step):
        RXG[step, si] = GS[...]
        return exchange(RXG, step, si, src_peers(), gsend, grecv, lambda p: (p, ti))

    def lse_of(buf, step, n):
        parts = [buf[step, k] for k in range(n)]
        top = functools.reduce(jnp.maximum, parts)
        return top + jnp.log2(sum(jnp.exp2(x - top) for x in parts))

    pending = []
    slw = slw_ref[...] * LOG2E
    tlw = tlw_ref[...] * LOG2E

    for c in range(rc):
        mt, st = M[tile(c), :].T, T[tile(c), :].T
        top = jnp.max(mt, axis=0, keepdims=True)
        FS[c : c + 1, :] = top + jnp.log2(jnp.sum(st * jnp.exp2(mt - top), axis=0, keepdims=True))
    pl.semaphore_wait(barrier, (n_src - 1) + (n_tgt - 1))
    pending += share_rows(0)
    f1 = slw - lse_of(RXF, 0, n_tgt)
    to_columns(f1)

    def peak_cols(r, acc):
        fb = FB[r, :]
        return tuple(jnp.maximum(a, S[r, tile(t)] + fb) for t, a in enumerate(acc))

    acc = groups(peak_cols, tuple(jnp.full((8, LANES), -jnp.inf, f32) for t in range(cc)), 4)
    for t in range(cc):
        GS[t : t + 1, :] = jnp.max(acc[t], axis=0, keepdims=True)
    cm = GS[...]
    less = [broadcast_down(SHIFT - cm[t : t + 1, :]) for t in range(cc)]

    def first_cols(r, acc):
        fb = FB[r, :]
        new = []
        for t, a in enumerate(acc):
            e = jnp.exp2(S[r, tile(t)] + fb + less[t])
            S[r, tile(t)] = e
            new.append(a + e)
        return tuple(new)

    zeros = tuple(jnp.zeros((8, LANES), f32) for t in range(cc))
    acc = groups(first_cols, zeros, 2)
    for t in range(cc):
        GS[t : t + 1, :] = jnp.sum(acc[t], axis=0, keepdims=True)
    GS[...] = cm + (jnp.log2(GS[...]) - SHIFT)
    pending += share_cols(0)
    g = tlw - lse_of(RXG, 0, n_src)
    v = jnp.exp2(cm + g)

    for step in range(1, ITERS):
        vb = [broadcast_down(v[t : t + 1, :]) for t in range(cc)]

        def later_rows(r, carry):
            parts = [S[r, tile(t)] * vb[t] for t in range(cc)]
            while len(parts) > 1:
                parts = [a + b for a, b in zip(parts[::2], parts[1::2])]
            T[r, :] = parts[0]
            return carry

        groups(later_rows, 0, 4)
        for c in range(rc):
            FS[c : c + 1, :] = jnp.sum(T[tile(c), :].T, axis=0, keepdims=True)
        pending += share_rows(step)
        move = slw + (SHIFT - jnp.log2(sum(RXF[step, k] for k in range(n_tgt))))
        u = jnp.exp2(move)
        to_columns(u)

        def later_cols(r, acc):
            ub = FB[r, :]
            return tuple(a + S[r, tile(t)] * ub for t, a in enumerate(acc))

        acc = groups(later_cols, zeros, 4)
        for t in range(cc):
            GS[t : t + 1, :] = jnp.sum(acc[t], axis=0, keepdims=True)
        GS[...] = GS[...] * v
        pending += share_cols(step)
        g = g + (tlw + (SHIFT - jnp.log2(sum(RXG[step, k] for k in range(n_src)))))
        v = jnp.exp2(cm + g)

    f_out[...] = (f1 + move) * LN2
    g_out[...] = g * LN2

    to_columns(u * (2.0 ** -SHIFT))
    tall = plan.shape[0]
    tgt = tgt_ref[...]
    total = None
    for c in range(rows // tall):
        at = slice(c * tall, (c + 1) * tall)
        ub = FB[at, :]
        for t in range(cc):
            plan[:, tile(t)] = (S[at, tile(t)] * ub * v[t : t + 1, :]).astype(bf16)
        panel = contract(plan[...], tgt, 1, 1)
        high = panel.astype(bf16)
        low = (panel - high.astype(f32)).astype(bf16)
        words = src_ref[:, at]
        part = jnp.dot(words, high, preferred_element_type=f32) + jnp.dot(
            words, low, preferred_element_type=f32
        )
        total = part if total is None else total + part

    full, rest = dim // LANES, dim % LANES
    line = -(-dim // 8) * 8
    short = -(-rest // 8) * 8
    CB[...] = jnp.zeros(CB.shape, f32)
    for t in range(full):
        CB[t * line : t * line + dim, :] = total[:, tile(t)]
    if rest:
        plan_rows = -(-dim // LANES) * LANES
        S[0:plan_rows, 0:LANES] = jnp.zeros((plan_rows, LANES), f32)
        S[0:dim, 0:rest] = total[:, full * LANES :]
        for k in range(plan_rows // LANES):
            base = full * line + k * short
            CB[base : base + short, :] = S[tile(k), 0:LANES].T[0:short, :]

    height = CB.shape[0]
    core_id, zi, nz = lax.rem(ti, 2), lax.div(ti, 2), n_tgt // 2
    half = height // 2
    quart = half // n_src
    piece = quart // nz
    half_at = core_id * half
    quart_at = half_at + si * quart
    piece_at = quart_at + zi * piece

    def span(start, size):
        return pl.ds(pl.multiple_of(start, 8), size)

    def remote(source, dest, send, recv, where):
        return pltpu.make_async_remote_copy(
            src_ref=source, dst_ref=dest, send_sem=send, recv_sem=recv,
            device_id=where, device_id_type=MESH,
        )

    mate = (si, zi * 2 + (1 - core_id))
    z_peers = [lax.rem(zi + k, nz) for k in range(1, nz)]
    on_z = lambda p: (si, p * 2 + core_id)
    on_src = lambda p: (p, ti)

    copy = remote(CB.at[span((1 - core_id) * half, half)], RX1, s1, r1, mate)
    copy.start()
    copy.wait_recv()
    pending.append(copy)
    CB[span(half_at, half), :] += RX1[...]

    def scatter(n, me, peers, base, size, RX, send, recv, where):
        for k, p in enumerate(peers):
            copy = remote(CB.at[span(base + p * size, size)], RX.at[me], send.at[k], recv.at[me], where(p))
            copy.start()
            pending.append(copy)
        for k, p in enumerate(peers):
            remote(RX.at[p], RX.at[p], send.at[k], recv.at[p], where(p)).wait_recv()
        own = CB[span(base + me * size, size), :]
        for p in peers:
            own = own + RX[p]
        return own

    CB[span(quart_at, quart), :] = scatter(n_src, si, src_peers(), half_at, quart, RX2, s2, r2, on_src)
    OUT[span(piece_at, piece), :] = scatter(nz, zi, z_peers, quart_at, piece, RX3, s3, r3, on_z)

    def gather(me, peers, base, size, send, recv, where):
        for k, p in enumerate(peers):
            at = span(base + me * size, size)
            copy = remote(OUT.at[at], OUT.at[at], send.at[k], recv.at[me], where(p))
            copy.start()
            pending.append(copy)
        for k, p in enumerate(peers):
            at = span(base + p * size, size)
            remote(OUT.at[at], OUT.at[at], send.at[k], recv.at[p], where(p)).wait_recv()

    gather(zi, z_peers, quart_at, piece, s4, r4, on_z)
    gather(si, src_peers(), half_at, quart, s5, r5, on_src)
    gather(core_id, [1 - core_id], 0, half, s6, r6, lambda p: mate)

    scale = dim / (rows * n_src)
    for t in range(full):
        core_out[:, tile(t)] = OUT[t * line : t * line + dim, :] * scale
    if rest:
        for k in range(-(-dim // LANES)):
            base = full * line + k * short
            CB_rows = jnp.concatenate(
                [OUT[base : base + short, :], jnp.zeros((LANES - short, LANES), f32)], axis=0
            ).T * scale
            count = min(LANES, dim - k * LANES)
            core_out[k * LANES : k * LANES + count, full * LANES :] = CB_rows[0:count, 0:rest]

    for copy in pending:
        copy.wait_send()


def per_device(n_src, n_tgt, src_emb_t, tgt_emb_t, core, src_logw, tgt_logw):
    dim, rows = src_emb_t.shape
    cols = tgt_emb_t.shape[1]
    f32 = jnp.float32
    line, short = -(-dim // 8) * 8, -(-(dim % LANES) // 8) * 8
    need = (dim // LANES) * line + -(-dim // LANES) * short
    step = 8 * n_src * n_tgt
    height = -(-need // step) * step
    half = height // 2
    quart = half // n_src
    nz = n_tgt // 2
    sems = pltpu.SemaphoreType.DMA
    vmem = pl.BlockSpec(memory_space=pltpu.VMEM)
    rc, cc = rows // LANES, cols // LANES
    f, g, new = pl.pallas_call(
        functools.partial(kernel, n_src, n_tgt),
        out_shape=(
            jax.ShapeDtypeStruct((rc, LANES), f32),
            jax.ShapeDtypeStruct((cc, LANES), f32),
            jax.ShapeDtypeStruct((dim, dim), f32),
        ),
        in_specs=[vmem] * 5,
        out_specs=(vmem,) * 3,
        scratch_shapes=[
            pltpu.VMEM((rows, cols), f32),
            pltpu.VMEM((rows, dim), jnp.bfloat16),
            pltpu.VMEM((rows, LANES), f32),
            pltpu.VMEM((rows, LANES), f32),
            pltpu.VMEM((rows, LANES), f32),
            pltpu.VMEM((rc, LANES), f32),
            pltpu.VMEM((cc, LANES), f32),
            pltpu.VMEM((ITERS, n_tgt, rc, LANES), f32),
            pltpu.VMEM((ITERS, n_src, cc, LANES), f32),
            pltpu.VMEM((256, cols), jnp.bfloat16),
            pltpu.VMEM((height, LANES), f32),
            pltpu.VMEM((half, LANES), f32),
            pltpu.VMEM((n_src, quart, LANES), f32),
            pltpu.VMEM((nz, quart // nz, LANES), f32),
            pltpu.VMEM((height, LANES), f32),
            sems((ITERS, n_tgt)), sems((ITERS, n_tgt)),
            sems((ITERS, n_src)), sems((ITERS, n_src)),
            sems, sems,
            sems((n_src,)), sems((n_src,)),
            sems((nz,)), sems((nz,)),
            sems((nz,)), sems((nz,)),
            sems((n_src,)), sems((n_src,)),
            sems((2,)), sems((2,)),
        ],
        compiler_params=pltpu.CompilerParams(
            collective_id=0, has_side_effects=True, vmem_limit_bytes=48 * 1024 * 1024
        ),
    )(src_emb_t, tgt_emb_t, core, src_logw.reshape(rc, LANES), tgt_logw.reshape(cc, LANES))
    return f.reshape(rows), g.reshape(cols), new


def solution(mesh):
    placed = (P(None, "src"), P(None, "tgt"), P(), P("src"), P("tgt"))
    body = functools.partial(per_device, mesh.shape["src"], mesh.shape["tgt"])
    return jax.shard_map(
        body, mesh=mesh, in_specs=placed, out_specs=(P("src"), P("tgt"), P()), check_vma=False
    )
```

```python
import functools

import jax
import jax.numpy as jnp
from jax import lax
from jax.experimental import pallas as pl
from jax.experimental.pallas import tpu as pltpu
from jax.sharding import PartitionSpec as P

ITERS = 3
LOG2E = 1.4426950408889634
LN2 = 0.6931471805599453
LANES = 128
SHIFT = 60.0
MESH = pl.DeviceIdType.MESH


def tile(t):
    return slice(t * LANES, (t + 1) * LANES)


def kernel(
    n_src, n_tgt,
    src_hbm, tgt_hbm, core_hbm, slw_hbm, tlw_hbm,
    OUT,
    src_ref, tgt_ref, core_ref, slw_ref, tlw_ref, load,
    S, proj, M, T, FB, FS, GS, RXF, RXG, W, CB, RX1, RX2, RX3,
    fsend, frecv, gsend, grecv, s1, r1, s2, r2, s3, r3, s4, r4, s5, r5, s6, r6,
):
    si, ti = lax.axis_index("src"), lax.axis_index("tgt")
    dim, rows = src_ref.shape
    cols = tgt_ref.shape[1]
    rc, cc = rows // LANES, cols // LANES
    f32, bf16 = jnp.float32, jnp.bfloat16

    def src_peers():
        return [lax.rem(si + k, n_src) for k in range(1, n_src)]

    def tgt_peers():
        return [lax.rem(ti + k, n_tgt) for k in range(1, n_tgt)]

    loads = [
        pltpu.make_async_copy(a, b, load.at[k])
        for k, (a, b) in enumerate(
            [(core_hbm, core_ref), (src_hbm, src_ref), (tgt_hbm, tgt_ref), (slw_hbm, slw_ref), (tlw_hbm, tlw_ref)]
        )
    ]
    for copy in loads:
        copy.start()

    barrier = pltpu.get_barrier_semaphore()
    for p in src_peers():
        pl.semaphore_signal(barrier, inc=1, device_id=(p, ti), device_id_type=MESH)
    for p in tgt_peers():
        pl.semaphore_signal(barrier, inc=1, device_id=(si, p), device_id_type=MESH)

    loads[0].wait()
    loads[1].wait()
    c32 = core_ref[...]
    c0 = c32.astype(bf16)
    left = c32 - c0.astype(f32)
    c1 = left.astype(bf16)
    c2 = (left - c1.astype(f32)).astype(bf16)
    src = src_ref[...]

    def contract(a, b, da, db):
        return lax.dot_general(a, b, (((da,), (db,)), ((), ())), preferred_element_type=f32)

    proj[...] = (
        contract(c0, src, 0, 0) + (contract(c1, src, 0, 0) + contract(c2, src, 0, 0))
    ).T.astype(bf16)
    for copy in loads[2:]:
        copy.wait()

    wide = 4 * LANES
    for t in range(cols // wide):
        at = slice(t * wide, (t + 1) * wide)
        y = jnp.dot(proj[...], tgt_ref[:, at], preferred_element_type=f32) * LOG2E
        S[:, at] = y
        parts = [y[:, k : k + LANES] for k in range(0, wide, LANES)]
        top = functools.reduce(jnp.maximum, parts)
        M[...] = top if t == 0 else jnp.maximum(M[...], top)

    def groups(body, carry, unroll):
        def step(i, carry):
            for k in range(unroll):
                carry = body(pl.ds(pl.multiple_of((i * unroll + k) * 8, 8), 8), carry)
            return carry

        return lax.fori_loop(0, rows // (8 * unroll), step, carry)

    def first_rows(r, carry):
        m = M[r, :]
        parts = [jnp.exp2(S[r, tile(t)] - m) for t in range(cc)]
        while len(parts) > 1:
            parts = [a + b for a, b in zip(parts[::2], parts[1::2])]
        T[r, :] = parts[0]
        return carry

    groups(first_rows, 0, 4)

    def broadcast_down(line):
        return jnp.broadcast_to(line, (8, LANES))

    def to_columns(dense):
        for c in range(rc):
            FB[tile(c), :] = jnp.broadcast_to(dense[c : c + 1, :], (LANES, LANES)).T

    def exchange(buf, step, me, peers, send, recv, where, meanwhile):
        for k, p in enumerate(peers):
            copy = pltpu.make_async_remote_copy(
                src_ref=buf.at[step, me],
                dst_ref=buf.at[step, me],
                send_sem=send.at[step, k],
                recv_sem=recv.at[step, me],
                device_id=where(p),
                device_id_type=MESH,
            )
            copy.start()
            pending.append(copy)
        if meanwhile is not None:
            meanwhile()
        for k, p in enumerate(peers):
            pltpu.make_async_remote_copy(
                src_ref=buf.at[step, p],
                dst_ref=buf.at[step, p],
                send_sem=send.at[step, k],
                recv_sem=recv.at[step, p],
                device_id=where(p),
                device_id_type=MESH,
            ).wait_recv()

    def share_rows(step, meanwhile=None):
        RXF[step, ti] = FS[...]
        exchange(RXF, step, ti, tgt_peers(), fsend, frecv, lambda p: (si, p), meanwhile)

    def share_cols(step, meanwhile=None):
        RXG[step, si] = GS[...]
        exchange(RXG, step, si, src_peers(), gsend, grecv, lambda p: (p, ti), meanwhile)

    def lse_of(buf, step, n):
        parts = [buf[step, k] for k in range(n)]
        top = functools.reduce(jnp.maximum, parts)
        return top + jnp.log2(sum(jnp.exp2(x - top) for x in parts))

    pending = []
    slw = slw_ref[...] * LOG2E
    tlw = tlw_ref[...] * LOG2E

    for c in range(rc):
        mt, st = M[tile(c), :].T, T[tile(c), :].T
        top = jnp.max(mt, axis=0, keepdims=True)
        FS[c : c + 1, :] = top + jnp.log2(jnp.sum(st * jnp.exp2(mt - top), axis=0, keepdims=True))
    pl.semaphore_wait(barrier, (n_src - 1) + (n_tgt - 1))
    share_rows(0)
    f1 = slw - lse_of(RXF, 0, n_tgt)
    to_columns(f1)

    def peak_cols(r, acc):
        fb = FB[r, :]
        return tuple(jnp.maximum(a, S[r, tile(t)] + fb) for t, a in enumerate(acc))

    acc = groups(peak_cols, tuple(jnp.full((8, LANES), -jnp.inf, f32) for t in range(cc)), 4)
    for t in range(cc):
        GS[t : t + 1, :] = jnp.max(acc[t], axis=0, keepdims=True)
    cm = GS[...]
    less = [broadcast_down(SHIFT - cm[t : t + 1, :]) for t in range(cc)]

    def first_cols(r, acc):
        fb = FB[r, :]
        new = []
        for t, a in enumerate(acc):
            e = jnp.exp2(S[r, tile(t)] + fb + less[t])
            S[r, tile(t)] = e
            new.append(a + e)
        return tuple(new)

    zeros = tuple(jnp.zeros((8, LANES), f32) for t in range(cc))
    acc = groups(first_cols, zeros, 2)
    for t in range(cc):
        GS[t : t + 1, :] = jnp.sum(acc[t], axis=0, keepdims=True)
    GS[...] = cm + (jnp.log2(GS[...]) - SHIFT)
    share_cols(0)
    g = tlw - lse_of(RXG, 0, n_src)
    v = jnp.exp2(cm + g)

    for step in range(1, ITERS):
        vb = [broadcast_down(v[t : t + 1, :]) for t in range(cc)]

        def later_rows(r, carry):
            parts = [S[r, tile(t)] * vb[t] for t in range(cc)]
            while len(parts) > 1:
                parts = [a + b for a, b in zip(parts[::2], parts[1::2])]
            T[r, :] = parts[0]
            return carry

        groups(later_rows, 0, 4)
        for c in range(rc):
            FS[c : c + 1, :] = jnp.sum(T[tile(c), :].T, axis=0, keepdims=True)
        share_rows(step)
        move = slw - jnp.log2(sum(RXF[step, k] for k in range(n_tgt)))
        to_columns(jnp.exp2(move))
        last = step == ITERS - 1

        def later_cols(r, acc):
            ub = FB[r, :]
            new = []
            for t, a in enumerate(acc):
                e = S[r, tile(t)] * ub
                if last:
                    S[r, tile(t)] = e
                new.append(a + e)
            return tuple(new)

        acc = groups(later_cols, zeros, 4)
        for t in range(cc):
            GS[t : t + 1, :] = jnp.sum(acc[t], axis=0, keepdims=True)
        GS[...] = GS[...] * v

        def source_sums():
            for t in range(0, cols, 2 * LANES):
                at = slice(t, t + 2 * LANES)
                W[:, at] = jnp.dot(src_ref[...], S[:, at].astype(bf16), preferred_element_type=f32)

        share_cols(step, source_sums if last else None)
        g = g + (tlw - jnp.log2(sum(RXG[step, k] for k in range(n_src))))
        v = jnp.exp2(cm + g)

    height = CB.shape[0]
    OUT[height : height + rc, :] = (f1 + (move + SHIFT)) * LN2
    OUT[height + rc : height + rc + cc, :] = g * LN2

    total = None
    for t in range(0, cc, 4):
        at = slice(t * LANES, (t + 4) * LANES)
        x = jnp.concatenate([W[:, tile(k)] * v[k : k + 1, :] for k in range(t, t + 4)], axis=1)
        high = x.astype(bf16)
        low = (x - high.astype(f32)).astype(bf16)
        words = tgt_ref[:, at]
        part = contract(high, words, 1, 1) + contract(low, words, 1, 1)
        total = part if total is None else total + part

    full, rest = dim // LANES, dim % LANES
    line = -(-dim // 8) * 8
    short = -(-rest // 8) * 8
    CB[...] = jnp.zeros(CB.shape, f32)
    for t in range(full):
        CB[t * line : t * line + dim, :] = total[:, tile(t)]
    if rest:
        plan_rows = -(-dim // LANES) * LANES
        S[0:plan_rows, 0:LANES] = jnp.zeros((plan_rows, LANES), f32)
        S[0:dim, 0:rest] = total[:, full * LANES :]
        for k in range(plan_rows // LANES):
            base = full * line + k * short
            CB[base : base + short, :] = S[tile(k), 0:LANES].T[0:short, :]

    core_id, zi, nz = lax.rem(ti, 2), lax.div(ti, 2), n_tgt // 2
    half = height // 2
    quart = half // n_src
    piece = quart // nz
    half_at = core_id * half
    quart_at = half_at + si * quart
    piece_at = quart_at + zi * piece

    def span(start, size):
        return pl.ds(pl.multiple_of(start, 8), size)

    def remote(source, dest, send, recv, where):
        return pltpu.make_async_remote_copy(
            src_ref=source, dst_ref=dest, send_sem=send, recv_sem=recv,
            device_id=where, device_id_type=MESH,
        )

    mate = (si, zi * 2 + (1 - core_id))
    z_peers = [lax.rem(zi + k, nz) for k in range(1, nz)]
    on_z = lambda p: (si, p * 2 + core_id)
    on_src = lambda p: (p, ti)

    copy = remote(CB.at[span((1 - core_id) * half, half)], RX1, s1, r1, mate)
    copy.start()
    copy.wait_recv()
    pending.append(copy)
    CB[span(half_at, half), :] += RX1[...]

    def scatter(n, me, peers, base, size, RX, send, recv, where):
        for k, p in enumerate(peers):
            copy = remote(CB.at[span(base + p * size, size)], RX.at[me], send.at[k], recv.at[me], where(p))
            copy.start()
            pending.append(copy)
        for k, p in enumerate(peers):
            remote(RX.at[p], RX.at[p], send.at[k], recv.at[p], where(p)).wait_recv()
        own = CB[span(base + me * size, size), :]
        for p in peers:
            own = own + RX[p]
        return own

    CB[span(quart_at, quart), :] = scatter(n_src, si, src_peers(), half_at, quart, RX2, s2, r2, on_src)
    OUT[span(piece_at, piece), :] = scatter(nz, zi, z_peers, quart_at, piece, RX3, s3, r3, on_z)

    def gather(me, peers, base, size, send, recv, where):
        for k, p in enumerate(peers):
            at = span(base + me * size, size)
            copy = remote(OUT.at[at], OUT.at[at], send.at[k], recv.at[me], where(p))
            copy.start()
            pending.append(copy)
        for k, p in enumerate(peers):
            at = span(base + p * size, size)
            remote(OUT.at[at], OUT.at[at], send.at[k], recv.at[p], where(p)).wait_recv()

    gather(zi, z_peers, quart_at, piece, s4, r4, on_z)
    gather(si, src_peers(), half_at, quart, s5, r5, on_src)
    gather(core_id, [1 - core_id], 0, half, s6, r6, lambda p: mate)

    for copy in pending:
        copy.wait_send()


def unpack(scale, dim, height, lines, f_out, g_out, core_out):
    rc, cc = f_out.shape[0], g_out.shape[0]
    f_out[...] = lines[height : height + rc, :]
    g_out[...] = lines[height + rc : height + rc + cc, :]
    full, rest = dim // LANES, dim % LANES
    line = -(-dim // 8) * 8
    short = -(-rest // 8) * 8
    for t in range(full):
        core_out[:, tile(t)] = lines[t * line : t * line + dim, :] * scale
    if rest:
        for k in range(-(-dim // LANES)):
            base = full * line + k * short
            block = jnp.concatenate(
                [lines[base : base + short, :], jnp.zeros((LANES - short, LANES), jnp.float32)], axis=0
            ).T * scale
            count = min(LANES, dim - k * LANES)
            core_out[k * LANES : k * LANES + count, full * LANES :] = block[0:count, 0:rest]


def per_device(n_src, n_tgt, src_emb_t, tgt_emb_t, core, src_logw, tgt_logw):
    dim, rows = src_emb_t.shape
    cols = tgt_emb_t.shape[1]
    f32 = jnp.float32
    line, short = -(-dim // 8) * 8, -(-(dim % LANES) // 8) * 8
    need = (dim // LANES) * line + -(-dim // LANES) * short
    step = 8 * n_src * n_tgt
    height = -(-need // step) * step
    half = height // 2
    quart = half // n_src
    nz = n_tgt // 2
    sems = pltpu.SemaphoreType.DMA
    vmem = pl.BlockSpec(memory_space=pltpu.VMEM)
    rc, cc = rows // LANES, cols // LANES
    hbm = pl.BlockSpec(memory_space=pltpu.HBM)
    lines = pl.pallas_call(
        functools.partial(kernel, n_src, n_tgt),
        out_shape=jax.ShapeDtypeStruct((height + rc + cc, LANES), f32),
        in_specs=[hbm] * 5,
        out_specs=vmem,
        scratch_shapes=[
            pltpu.VMEM(src_emb_t.shape, jnp.bfloat16),
            pltpu.VMEM(tgt_emb_t.shape, jnp.bfloat16),
            pltpu.VMEM(core.shape, f32),
            pltpu.VMEM((rc, LANES), f32),
            pltpu.VMEM((cc, LANES), f32),
            sems((5,)),
            pltpu.VMEM((rows, cols), f32),
            pltpu.VMEM((rows, dim), jnp.bfloat16),
            pltpu.VMEM((rows, LANES), f32),
            pltpu.VMEM((rows, LANES), f32),
            pltpu.VMEM((rows, LANES), f32),
            pltpu.VMEM((rc, LANES), f32),
            pltpu.VMEM((cc, LANES), f32),
            pltpu.VMEM((ITERS, n_tgt, rc, LANES), f32),
            pltpu.VMEM((ITERS, n_src, cc, LANES), f32),
            pltpu.VMEM((dim, cols), f32),
            pltpu.VMEM((height, LANES), f32),
            pltpu.VMEM((half, LANES), f32),
            pltpu.VMEM((n_src, quart, LANES), f32),
            pltpu.VMEM((nz, quart // nz, LANES), f32),
            sems((ITERS, n_tgt)), sems((ITERS, n_tgt)),
            sems((ITERS, n_src)), sems((ITERS, n_src)),
            sems, sems,
            sems((n_src,)), sems((n_src,)),
            sems((nz,)), sems((nz,)),
            sems((nz,)), sems((nz,)),
            sems((n_src,)), sems((n_src,)),
            sems((2,)), sems((2,)),
        ],
        compiler_params=pltpu.CompilerParams(
            collective_id=0, has_side_effects=True, vmem_limit_bytes=64 * 1024 * 1024
        ),
    )(src_emb_t, tgt_emb_t, core, src_logw.reshape(rc, LANES), tgt_logw.reshape(cc, LANES))
    f, g, new = pl.pallas_call(
        functools.partial(unpack, dim / (rows * n_src), dim, height),
        out_shape=(
            jax.ShapeDtypeStruct((rc, LANES), f32),
            jax.ShapeDtypeStruct((cc, LANES), f32),
            jax.ShapeDtypeStruct((dim, dim), f32),
        ),
        in_specs=[vmem],
        out_specs=(vmem,) * 3,
        compiler_params=pltpu.CompilerParams(vmem_limit_bytes=64 * 1024 * 1024),
    )(lines)
    return f.reshape(rows), g.reshape(cols), new


def solution(mesh):
    placed = (P(None, "src"), P(None, "tgt"), P(), P("src"), P("tgt"))
    body = functools.partial(per_device, mesh.shape["src"], mesh.shape["tgt"])
    return jax.shard_map(
        body, mesh=mesh, in_specs=placed, out_specs=(P("src"), P("tgt"), P()), check_vma=False
    )
```

```python
import functools

import jax
import jax.numpy as jnp
from jax import lax
from jax.experimental import pallas as pl
from jax.experimental.pallas import tpu as pltpu
from jax.sharding import PartitionSpec as P

ITERS = 3
LOG2E = 1.4426950408889634
LN2 = 0.6931471805599453
LANES = 128
SHIFT = 60.0
MESH = pl.DeviceIdType.MESH


def tile(t):
    return slice(t * LANES, (t + 1) * LANES)


def kernel(
    n_src, n_tgt,
    src_hbm, tgt_hbm, core_hbm, slw_hbm, tlw_hbm,
    OUT,
    src_ref, tgt_ref, core_ref, slw_ref, tlw_ref, load,
    S, proj, M, T, FB, FS, GS, RXF, RXG, W, CB, RX1, RX2a, RX3a, RX2b, RX3b,
    fsend, frecv, gsend, grecv, s1, r1, s2, r2,
):
    si, ti = lax.axis_index("src"), lax.axis_index("tgt")
    dim, rows = src_ref.shape
    cols = tgt_ref.shape[1]
    rc, cc = rows // LANES, cols // LANES
    f32, bf16 = jnp.float32, jnp.bfloat16

    def src_peers():
        return [lax.rem(si + k, n_src) for k in range(1, n_src)]

    def tgt_peers():
        return [lax.rem(ti + k, n_tgt) for k in range(1, n_tgt)]

    loads = [
        pltpu.make_async_copy(a, b, load.at[k])
        for k, (a, b) in enumerate(
            [(core_hbm, core_ref), (src_hbm, src_ref), (tgt_hbm, tgt_ref), (slw_hbm, slw_ref), (tlw_hbm, tlw_ref)]
        )
    ]
    for copy in loads:
        copy.start()

    barrier = pltpu.get_barrier_semaphore()
    for p in src_peers():
        pl.semaphore_signal(barrier, inc=1, device_id=(p, ti), device_id_type=MESH)
    for p in tgt_peers():
        pl.semaphore_signal(barrier, inc=1, device_id=(si, p), device_id_type=MESH)

    loads[0].wait()
    loads[1].wait()
    c32 = core_ref[...]
    c0 = c32.astype(bf16)
    c1 = (c32 - c0.astype(f32)).astype(bf16)
    src = src_ref[...]

    def contract(a, b, da, db):
        return lax.dot_general(a, b, (((da,), (db,)), ((), ())), preferred_element_type=f32)

    proj[...] = (
        contract(c0, src, 0, 0) + contract(c1, src, 0, 0)
    ).T.astype(bf16)
    for copy in loads[2:]:
        copy.wait()

    wide = 4 * LANES
    for t in range(cols // wide):
        at = slice(t * wide, (t + 1) * wide)
        y = jnp.dot(proj[...], tgt_ref[:, at], preferred_element_type=f32) * LOG2E
        S[:, at] = y
        parts = [y[:, k : k + LANES] for k in range(0, wide, LANES)]
        top = functools.reduce(jnp.maximum, parts)
        M[...] = top if t == 0 else jnp.maximum(M[...], top)

    def groups(body, carry, unroll):
        def step(i, carry):
            for k in range(unroll):
                carry = body(pl.ds(pl.multiple_of((i * unroll + k) * 8, 8), 8), carry)
            return carry

        return lax.fori_loop(0, rows // (8 * unroll), step, carry)

    def first_rows(r, carry):
        m = M[r, :]
        parts = [jnp.exp2(S[r, tile(t)] - m) for t in range(cc)]
        while len(parts) > 1:
            parts = [a + b for a, b in zip(parts[::2], parts[1::2])]
        T[r, :] = parts[0]
        return carry

    groups(first_rows, 0, 4)

    def broadcast_down(line):
        return jnp.broadcast_to(line, (8, LANES))

    def to_columns(dense):
        for c in range(rc):
            FB[tile(c), :] = jnp.broadcast_to(dense[c : c + 1, :], (LANES, LANES)).T

    def exchange(buf, step, me, peers, send, recv, where, meanwhile):
        for k, p in enumerate(peers):
            copy = pltpu.make_async_remote_copy(
                src_ref=buf.at[step, me],
                dst_ref=buf.at[step, me],
                send_sem=send.at[step, k],
                recv_sem=recv.at[step, me],
                device_id=where(p),
                device_id_type=MESH,
            )
            copy.start()
            pending.append(copy)
        if meanwhile is not None:
            meanwhile()
        for k, p in enumerate(peers):
            pltpu.make_async_remote_copy(
                src_ref=buf.at[step, p],
                dst_ref=buf.at[step, p],
                send_sem=send.at[step, k],
                recv_sem=recv.at[step, p],
                device_id=where(p),
                device_id_type=MESH,
            ).wait_recv()

    def share_rows(step, meanwhile=None):
        RXF[step, ti] = FS[...]
        exchange(RXF, step, ti, tgt_peers(), fsend, frecv, lambda p: (si, p), meanwhile)

    def share_cols(step, meanwhile=None):
        RXG[step, si] = GS[...]
        exchange(RXG, step, si, src_peers(), gsend, grecv, lambda p: (p, ti), meanwhile)

    def lse_of(buf, step, n):
        parts = [buf[step, k] for k in range(n)]
        top = functools.reduce(jnp.maximum, parts)
        return top + jnp.log2(sum(jnp.exp2(x - top) for x in parts))

    pending = []
    slw = slw_ref[...] * LOG2E
    tlw = tlw_ref[...] * LOG2E

    for c in range(rc):
        mt, st = M[tile(c), :].T, T[tile(c), :].T
        top = jnp.max(mt, axis=0, keepdims=True)
        FS[c : c + 1, :] = top + jnp.log2(jnp.sum(st * jnp.exp2(mt - top), axis=0, keepdims=True))
    pl.semaphore_wait(barrier, (n_src - 1) + (n_tgt - 1))
    share_rows(0)
    f1 = slw - lse_of(RXF, 0, n_tgt)
    to_columns(f1)

    def peak_cols(r, acc):
        fb = FB[r, :]
        return tuple(jnp.maximum(a, S[r, tile(t)] + fb) for t, a in enumerate(acc))

    acc = groups(peak_cols, tuple(jnp.full((8, LANES), -jnp.inf, f32) for t in range(cc)), 4)
    for t in range(cc):
        GS[t : t + 1, :] = jnp.max(acc[t], axis=0, keepdims=True)
    cm = GS[...]
    less = [broadcast_down(SHIFT - cm[t : t + 1, :]) for t in range(cc)]

    def first_cols(r, acc):
        fb = FB[r, :]
        new = []
        for t, a in enumerate(acc):
            e = jnp.exp2(S[r, tile(t)] + fb + less[t])
            S[r, tile(t)] = e
            new.append(a + e)
        return tuple(new)

    zeros = tuple(jnp.zeros((8, LANES), f32) for t in range(cc))
    acc = groups(first_cols, zeros, 2)
    for t in range(cc):
        GS[t : t + 1, :] = jnp.sum(acc[t], axis=0, keepdims=True)
    GS[...] = cm + (jnp.log2(GS[...]) - SHIFT)
    share_cols(0)
    g = tlw - lse_of(RXG, 0, n_src)
    v = jnp.exp2(cm + g)

    for step in range(1, ITERS):
        vb = [broadcast_down(v[t : t + 1, :]) for t in range(cc)]

        def later_rows(r, carry):
            parts = [S[r, tile(t)] * vb[t] for t in range(cc)]
            while len(parts) > 1:
                parts = [a + b for a, b in zip(parts[::2], parts[1::2])]
            T[r, :] = parts[0]
            return carry

        groups(later_rows, 0, 4)
        for c in range(rc):
            FS[c : c + 1, :] = jnp.sum(T[tile(c), :].T, axis=0, keepdims=True)
        share_rows(step)
        move = slw - jnp.log2(sum(RXF[step, k] for k in range(n_tgt)))
        to_columns(jnp.exp2(move))
        last = step == ITERS - 1

        def later_cols(r, acc):
            ub = FB[r, :]
            new = []
            for t, a in enumerate(acc):
                e = S[r, tile(t)] * ub
                if last:
                    S[r, tile(t)] = e
                new.append(a + e)
            return tuple(new)

        acc = groups(later_cols, zeros, 4)
        for t in range(cc):
            GS[t : t + 1, :] = jnp.sum(acc[t], axis=0, keepdims=True)
        GS[...] = GS[...] * v

        def source_sums():
            for t in range(0, cols, 2 * LANES):
                at = slice(t, t + 2 * LANES)
                W[:, at] = jnp.dot(src_ref[...], S[:, at].astype(bf16), preferred_element_type=f32)

        share_cols(step, source_sums if last else None)
        g = g + (tlw - jnp.log2(sum(RXG[step, k] for k in range(n_src))))
        v = jnp.exp2(cm + g)

    height = CB.shape[0]
    OUT[height : height + rc, :] = (f1 + (move + SHIFT)) * LN2
    OUT[height + rc : height + rc + cc, :] = g * LN2

    total = None
    for t in range(0, cc, 4):
        at = slice(t * LANES, (t + 4) * LANES)
        x = jnp.concatenate([W[:, tile(k)] * v[k : k + 1, :] for k in range(t, t + 4)], axis=1)
        part = contract(x.astype(bf16), tgt_ref[:, at], 1, 1)
        total = part if total is None else total + part

    full, rest = dim // LANES, dim % LANES
    line = -(-dim // 8) * 8
    short = -(-rest // 8) * 8
    CB[...] = jnp.zeros(CB.shape, f32)
    for t in range(full):
        CB[t * line : t * line + dim, :] = total[:, tile(t)]
    if rest:
        plan_rows = -(-dim // LANES) * LANES
        S[0:plan_rows, 0:LANES] = jnp.zeros((plan_rows, LANES), f32)
        S[0:dim, 0:rest] = total[:, full * LANES :]
        for k in range(plan_rows // LANES):
            base = full * line + k * short
            CB[base : base + short, :] = S[tile(k), 0:LANES].T[0:short, :]

    core_id, zi, nz = lax.rem(ti, 2), lax.div(ti, 2), n_tgt // 2
    half = height // 2
    mate = (si, zi * 2 + (1 - core_id))
    on_src = (n_src, si, src_peers(), lambda p: (p, ti))
    on_z = (nz, zi, [lax.rem(zi + k, nz) for k in range(1, nz)], lambda p: (si, p * 2 + core_id))
    streams = [(0, half * 2 // 3, on_src, on_z, RX2a, RX3a), (half * 2 // 3, half // 3, on_z, on_src, RX2b, RX3b)]

    def span(start, size):
        return pl.ds(pl.multiple_of(start, 8), size)

    def remote(source, dest, send, recv, where):
        return pltpu.make_async_remote_copy(
            src_ref=source, dst_ref=dest, send_sem=send, recv_sem=recv,
            device_id=where, device_id_type=MESH,
        )

    def post(source, dest, send, recv, where):
        copy = remote(source, dest, send, recv, where)
        copy.start()
        pending.append(copy)

    for w, (start, size, *_) in enumerate(streams):
        theirs = span((1 - core_id) * half + start, size)
        post(CB.at[theirs], RX1.at[start : start + size], s1.at[w], r1.at[w], mate)

    def post_scatter(w, stage, group, base, size, RX):
        n, me, peers, where = group
        for k, p in enumerate(peers):
            post(CB.at[span(base + p * size, size)], RX.at[me], s2.at[w, stage, k], r2.at[w, stage, me], where(p))

    def end_scatter(w, stage, group, base, size, RX):
        n, me, peers, where = group
        own = CB[span(base + me * size, size), :]
        for k, p in enumerate(peers):
            remote(RX.at[p], RX.at[p], s2.at[w, stage, k], r2.at[w, stage, p], where(p)).wait_recv()
            own = own + RX[p]
        return own

    def post_gather(w, stage, group, base, size):
        n, me, peers, where = group
        at = span(base + me * size, size)
        for k, p in enumerate(peers):
            post(OUT.at[at], OUT.at[at], s2.at[w, stage, k], r2.at[w, stage, me], where(p))

    def wait_block(w, stage, k, p, at, where):
        remote(OUT.at[at], OUT.at[at], s2.at[w, stage, k], r2.at[w, stage, p], where).wait_recv()

    plans = []
    for w, (start, size, first, second, RXa, RXb) in enumerate(streams):
        base = core_id * half + start
        block = size // first[0]
        block_at = base + first[1] * block
        piece = block // second[0]
        plans.append((base, block, block_at, piece))
        at = span(base, size)
        remote(CB.at[at], RX1.at[start : start + size], s1.at[w], r1.at[w], mate).wait_recv()
        CB[at, :] += RX1[start : start + size, :]
        post_scatter(w, 0, first, base, block, RXa)
    for w, (start, size, first, second, RXa, RXb) in enumerate(streams):
        base, block, block_at, piece = plans[w]
        CB[span(block_at, block), :] = end_scatter(w, 0, first, base, block, RXa)
        post_scatter(w, 1, second, block_at, piece, RXb)
    for w, (start, size, first, second, RXa, RXb) in enumerate(streams):
        base, block, block_at, piece = plans[w]
        OUT[span(block_at + second[1] * piece, piece), :] = end_scatter(w, 1, second, block_at, piece, RXb)
        post_gather(w, 2, second, block_at, piece)
    for w, (start, size, first, second, RXa, RXb) in enumerate(streams):
        base, block, block_at, piece = plans[w]
        for k, p in enumerate(second[2]):
            wait_block(w, 2, k, p, span(block_at + p * piece, piece), second[3](p))
        post_gather(w, 3, first, base, block)
        at = span(block_at, block)
        post(OUT.at[at], OUT.at[at], s2.at[w, 4, first[0] - 1], r2.at[w, 4, first[1]], mate)
    for w, (start, size, first, second, RXa, RXb) in enumerate(streams):
        base, block, block_at, piece = plans[w]
        for k, p in enumerate(first[2]):
            at = span(base + p * block, block)
            wait_block(w, 3, k, p, at, first[3](p))
            post(OUT.at[at], OUT.at[at], s2.at[w, 4, k], r2.at[w, 4, p], mate)
    for w, (start, size, first, second, RXa, RXb) in enumerate(streams):
        base, block, block_at, piece = plans[w]
        for p in range(first[0]):
            at = span((1 - core_id) * half + start + p * block, block)
            wait_block(w, 4, p, p, at, mate)

    for copy in pending:
        copy.wait_send()


def unpack(scale, dim, height, lines, f_out, g_out, core_out):
    rc, cc = f_out.shape[0], g_out.shape[0]
    f_out[...] = lines[height : height + rc, :]
    g_out[...] = lines[height + rc : height + rc + cc, :]
    full, rest = dim // LANES, dim % LANES
    line = -(-dim // 8) * 8
    short = -(-rest // 8) * 8
    for t in range(full):
        core_out[:, tile(t)] = lines[t * line : t * line + dim, :] * scale
    if rest:
        for k in range(-(-dim // LANES)):
            base = full * line + k * short
            block = jnp.concatenate(
                [lines[base : base + short, :], jnp.zeros((LANES - short, LANES), jnp.float32)], axis=0
            ).T * scale
            count = min(LANES, dim - k * LANES)
            core_out[k * LANES : k * LANES + count, full * LANES :] = block[0:count, 0:rest]


def per_device(n_src, n_tgt, src_emb_t, tgt_emb_t, core, src_logw, tgt_logw):
    dim, rows = src_emb_t.shape
    cols = tgt_emb_t.shape[1]
    f32 = jnp.float32
    line, short = -(-dim // 8) * 8, -(-(dim % LANES) // 8) * 8
    need = (dim // LANES) * line + -(-dim // LANES) * short
    nz = n_tgt // 2
    unit = 8 * n_src * nz
    half = -(-need // (6 * unit)) * 3 * unit
    height = 2 * half
    long, brief = half * 2 // 3, half // 3
    sems = pltpu.SemaphoreType.DMA
    vmem = pl.BlockSpec(memory_space=pltpu.VMEM)
    rc, cc = rows // LANES, cols // LANES
    hbm = pl.BlockSpec(memory_space=pltpu.HBM)
    lines = pl.pallas_call(
        functools.partial(kernel, n_src, n_tgt),
        out_shape=jax.ShapeDtypeStruct((height + rc + cc, LANES), f32),
        in_specs=[hbm] * 5,
        out_specs=vmem,
        scratch_shapes=[
            pltpu.VMEM(src_emb_t.shape, jnp.bfloat16),
            pltpu.VMEM(tgt_emb_t.shape, jnp.bfloat16),
            pltpu.VMEM(core.shape, f32),
            pltpu.VMEM((rc, LANES), f32),
            pltpu.VMEM((cc, LANES), f32),
            sems((5,)),
            pltpu.VMEM((rows, cols), f32),
            pltpu.VMEM((rows, dim), jnp.bfloat16),
            pltpu.VMEM((rows, LANES), f32),
            pltpu.VMEM((rows, LANES), f32),
            pltpu.VMEM((rows, LANES), f32),
            pltpu.VMEM((rc, LANES), f32),
            pltpu.VMEM((cc, LANES), f32),
            pltpu.VMEM((ITERS, n_tgt, rc, LANES), f32),
            pltpu.VMEM((ITERS, n_src, cc, LANES), f32),
            pltpu.VMEM((dim, cols), f32),
            pltpu.VMEM((height, LANES), f32),
            pltpu.VMEM((half, LANES), f32),
            pltpu.VMEM((n_src, long // n_src, LANES), f32),
            pltpu.VMEM((nz, long // (n_src * nz), LANES), f32),
            pltpu.VMEM((nz, brief // nz, LANES), f32),
            pltpu.VMEM((n_src, brief // (n_src * nz), LANES), f32),
            sems((ITERS, n_tgt)), sems((ITERS, n_tgt)),
            sems((ITERS, n_src)), sems((ITERS, n_src)),
            sems((2,)), sems((2,)),
            sems((2, 5, max(n_src, nz))), sems((2, 5, max(n_src, nz))),
        ],
        compiler_params=pltpu.CompilerParams(
            collective_id=0, has_side_effects=True, vmem_limit_bytes=64 * 1024 * 1024
        ),
    )(src_emb_t, tgt_emb_t, core, src_logw.reshape(rc, LANES), tgt_logw.reshape(cc, LANES))
    f, g, new = pl.pallas_call(
        functools.partial(unpack, dim / (rows * n_src), dim, height),
        out_shape=(
            jax.ShapeDtypeStruct((rc, LANES), f32),
            jax.ShapeDtypeStruct((cc, LANES), f32),
            jax.ShapeDtypeStruct((dim, dim), f32),
        ),
        in_specs=[vmem],
        out_specs=(vmem,) * 3,
        compiler_params=pltpu.CompilerParams(vmem_limit_bytes=64 * 1024 * 1024),
    )(lines)
    return f.reshape(rows), g.reshape(cols), new


def solution(mesh):
    placed = (P(None, "src"), P(None, "tgt"), P(), P("src"), P("tgt"))
    body = functools.partial(per_device, mesh.shape["src"], mesh.shape["tgt"])
    return jax.shard_map(
        body, mesh=mesh, in_specs=placed, out_specs=(P("src"), P("tgt"), P()), check_vma=False
    )
```

```python
import functools

import jax
import jax.numpy as jnp
from jax import lax
from jax.experimental import pallas as pl
from jax.experimental.pallas import tpu as pltpu
from jax.sharding import PartitionSpec as P

ITERS = 3
BLOCKS = 2
LOG2E = 1.4426950408889634
LN2 = 0.6931471805599453
LANES = 128
SHIFT = 60.0
MESH = pl.DeviceIdType.MESH


def tile(t):
    return slice(t * LANES, (t + 1) * LANES)


def kernel(
    n_src, n_tgt,
    src_hbm, tgt_hbm, core_hbm, slw_hbm, tlw_hbm,
    OUT,
    src_ref, tgt_ref, core_ref, slw_ref, tlw_ref, load,
    S, proj, M, T, FB, FS, GS, RXF, RXG, W, CB, RX1, RX2a, RX3a, RX2b, RX3b,
    fsend, frecv, gsend, grecv, s1, r1, s2, r2,
):
    si, ti = lax.axis_index("src"), lax.axis_index("tgt")
    dim, rows = src_ref.shape
    cols = tgt_ref.shape[1]
    rc, cc = rows // LANES, cols // LANES
    f32, bf16 = jnp.float32, jnp.bfloat16

    def src_peers():
        return [lax.rem(si + k, n_src) for k in range(1, n_src)]

    def tgt_peers():
        return [lax.rem(ti + k, n_tgt) for k in range(1, n_tgt)]

    loads = [
        pltpu.make_async_copy(a, b, load.at[k])
        for k, (a, b) in enumerate(
            [(core_hbm, core_ref), (src_hbm, src_ref), (tgt_hbm, tgt_ref), (slw_hbm, slw_ref), (tlw_hbm, tlw_ref)]
        )
    ]
    for copy in loads:
        copy.start()

    barrier = pltpu.get_barrier_semaphore()
    for p in src_peers():
        pl.semaphore_signal(barrier, inc=1, device_id=(p, ti), device_id_type=MESH)
    for p in tgt_peers():
        pl.semaphore_signal(barrier, inc=1, device_id=(si, p), device_id_type=MESH)

    loads[0].wait()
    loads[1].wait()
    c32 = core_ref[...]
    c0 = c32.astype(bf16)
    c1 = (c32 - c0.astype(f32)).astype(bf16)
    src = src_ref[...]

    def contract(a, b, da, db):
        return lax.dot_general(a, b, (((da,), (db,)), ((), ())), preferred_element_type=f32)

    proj[...] = (
        contract(c0, src, 0, 0) + contract(c1, src, 0, 0)
    ).T.astype(bf16)
    for copy in loads[2:]:
        copy.wait()

    blocks = range(BLOCKS)
    tall, bc = rows // BLOCKS, rc // BLOCKS
    wide = 4 * LANES
    pending, old = [], []

    def groups(b, body, carry, unroll):
        def step(i, carry):
            for k in range(unroll):
                at = b * tall + (i * unroll + k) * 8
                carry = body(pl.ds(pl.multiple_of(at, 8), 8), carry)
            return carry

        return lax.fori_loop(0, tall // (8 * unroll), step, carry)

    def broadcast_down(line):
        return jnp.broadcast_to(line, (8, LANES))

    def block_tile(b, c):
        return slice(b * tall + c * LANES, b * tall + (c + 1) * LANES)

    def to_columns(b, dense):
        for c in range(bc):
            FB[block_tile(b, c), :] = jnp.broadcast_to(dense[c : c + 1, :], (LANES, LANES)).T

    def add_up(parts):
        while len(parts) > 1:
            parts = [a + b for a, b in zip(parts[::2], parts[1::2])]
        return parts[0]

    def post_all(buf, me, peers, send, recv, where):
        for p in peers:
            pltpu.make_async_remote_copy(
                src_ref=buf.at[me], dst_ref=buf.at[me], send_sem=send, recv_sem=recv,
                device_id=where(p), device_id_type=MESH,
            ).start()

    def whole_wait(ref, send, recv, where):
        return pltpu.make_async_remote_copy(
            src_ref=ref, dst_ref=ref, send_sem=send, recv_sem=recv, device_id=where, device_id_type=MESH
        )

    mate = (si, ti + 1 - 2 * lax.rem(ti, 2))

    def post_rows(step, b):
        RXF[step, b, ti] = FS[b]
        post_all(RXF.at[step, b], ti, tgt_peers(), fsend.at[step, b], frecv.at[step, b], lambda p: (si, p))

    def rows_wait(step, b):
        ref = RXF.at[step, b, pl.ds(0, n_tgt - 1)]
        return whole_wait(ref, fsend.at[step, b], frecv.at[step, b], mate)

    def post_cols(step):
        RXG[step, si] = GS[...]
        post_all(RXG.at[step], si, src_peers(), gsend.at[step], grecv.at[step], lambda p: (p, ti))

    def cols_wait(step):
        return whole_wait(RXG.at[step, pl.ds(0, n_src - 1)], gsend.at[step], grecv.at[step], mate)

    def lse(parts):
        top = functools.reduce(jnp.maximum, parts)
        return top + jnp.log2(sum(jnp.exp2(x - top) for x in parts))

    slw = slw_ref[...] * LOG2E
    tlw = tlw_ref[...] * LOG2E

    def slw_of(b):
        return slw[b * bc : (b + 1) * bc, :]

    for b in blocks:
        mine = slice(b * tall, (b + 1) * tall)
        for t in range(cols // wide):
            at = slice(t * wide, (t + 1) * wide)
            y = jnp.dot(proj[mine, :], tgt_ref[:, at], preferred_element_type=f32) * LOG2E
            S[mine, at] = y
            top = functools.reduce(jnp.maximum, [y[:, k : k + LANES] for k in range(0, wide, LANES)])
            M[mine, :] = top if t == 0 else jnp.maximum(M[mine, :], top)

        def first_rows(r, carry):
            m = M[r, :]
            T[r, :] = add_up([jnp.exp2(S[r, tile(t)] - m) for t in range(cc)])
            return carry

        groups(b, first_rows, 0, 4)
        for c in range(bc):
            mt, st = M[block_tile(b, c), :].T, T[block_tile(b, c), :].T
            top = jnp.max(mt, axis=0, keepdims=True)
            FS[b, c : c + 1, :] = top + jnp.log2(jnp.sum(st * jnp.exp2(mt - top), axis=0, keepdims=True))
        if b == 0:
            pl.semaphore_wait(barrier, (n_src - 1) + (n_tgt - 1))
        post_rows(0, b)

    zeros = tuple(jnp.zeros((8, LANES), f32) for t in range(cc))
    f1, peaks, sums = [], [], []
    for b in blocks:
        rows_wait(0, b).wait_recv()
        f1.append(slw_of(b) - lse([RXF[0, b, k] for k in range(n_tgt)]))
        to_columns(b, f1[b])

        def peak_cols(r, acc):
            fb = FB[r, :]
            return tuple(jnp.maximum(a, S[r, tile(t)] + fb) for t, a in enumerate(acc))

        acc = groups(b, peak_cols, tuple(jnp.full((8, LANES), -jnp.inf, f32) for t in range(cc)), 4)
        for t in range(cc):
            GS[t : t + 1, :] = jnp.max(acc[t], axis=0, keepdims=True)
        peaks.append(GS[...])
        less = [broadcast_down(SHIFT - peaks[b][t : t + 1, :]) for t in range(cc)]

        def first_cols(r, acc):
            fb = FB[r, :]
            new = []
            for t, a in enumerate(acc):
                e = jnp.exp2(S[r, tile(t)] + fb + less[t])
                S[r, tile(t)] = e
                new.append(a + e)
            return tuple(new)

        acc = groups(b, first_cols, zeros, 2)
        for t in range(cc):
            GS[t : t + 1, :] = jnp.sum(acc[t], axis=0, keepdims=True)
        sums.append(peaks[b] + (jnp.log2(GS[...]) - SHIFT))
    GS[...] = lse(sums)
    post_cols(0)
    for b in blocks:
        rows_wait(0, b).wait_send()
    cols_wait(0).wait_recv()
    g = tlw - lse([RXG[0, k] for k in range(n_src)])
    v = [jnp.exp2(peaks[b] + g) for b in blocks]

    for step in range(1, ITERS):
        last = step == ITERS - 1
        for b in blocks:
            vb = [broadcast_down(v[b][t : t + 1, :]) for t in range(cc)]

            def later_rows(r, carry):
                T[r, :] = add_up([S[r, tile(t)] * vb[t] for t in range(cc)])
                return carry

            groups(b, later_rows, 0, 4)
            for c in range(bc):
                FS[b, c : c + 1, :] = jnp.sum(T[block_tile(b, c), :].T, axis=0, keepdims=True)
            post_rows(step, b)
        cols_wait(step - 1).wait_send()
        moves, sums = [], []
        for b in blocks:
            rows_wait(step, b).wait_recv()
            moves.append(slw_of(b) - jnp.log2(sum(RXF[step, b, k] for k in range(n_tgt))))
            to_columns(b, jnp.exp2(moves[b]))

            def later_cols(r, acc):
                ub = FB[r, :]
                new = []
                for t, a in enumerate(acc):
                    e = S[r, tile(t)] * ub
                    if last:
                        S[r, tile(t)] = e
                    new.append(a + e)
                return tuple(new)

            acc = groups(b, later_cols, zeros, 4)
            for t in range(cc):
                GS[t : t + 1, :] = jnp.sum(acc[t], axis=0, keepdims=True)
            sums.append(GS[...] * v[b])
        GS[...] = sum(sums)
        post_cols(step)
        for b in blocks:
            rows_wait(step, b).wait_send()
        if last:
            peak = functools.reduce(jnp.maximum, peaks)
            ratio = [jnp.exp2(peaks[b] - peak) for b in blocks]
            for t in range(0, cc, 2):
                at = slice(t * LANES, (t + 2) * LANES)
                whole = jnp.concatenate(
                    [
                        jnp.concatenate(
                            [
                                (S[b * tall : (b + 1) * tall, tile(k)] * ratio[b][k : k + 1, :]).astype(bf16)
                                for b in blocks
                            ],
                            axis=0,
                        )
                        for k in (t, t + 1)
                    ],
                    axis=1,
                )
                W[:, at] = jnp.dot(src_ref[...], whole, preferred_element_type=f32)
        cols_wait(step).wait_recv()
        g = g + (tlw - jnp.log2(sum(RXG[step, k] for k in range(n_src))))
        if not last:
            v = [jnp.exp2(peaks[b] + g) for b in blocks]

    end = jnp.exp2(peak + g)
    total = None
    for t in range(0, cc, 4):
        at = slice(t * LANES, (t + 4) * LANES)
        x = jnp.concatenate([W[:, tile(k)] * end[k : k + 1, :] for k in range(t, t + 4)], axis=1)
        part = contract(x.astype(bf16), tgt_ref[:, at], 1, 1)
        total = part if total is None else total + part

    height = CB.shape[0]
    full, rest = dim // LANES, dim % LANES
    line = -(-dim // 8) * 8
    short = -(-rest // 8) * 8
    CB[...] = jnp.zeros(CB.shape, f32)
    for t in range(full):
        CB[t * line : t * line + dim, :] = total[:, tile(t)]
    if rest:
        plan_rows = -(-dim // LANES) * LANES
        S[0:plan_rows, 0:LANES] = jnp.zeros((plan_rows, LANES), f32)
        S[0:dim, 0:rest] = total[:, full * LANES :]
        for k in range(plan_rows // LANES):
            base = full * line + k * short
            CB[base : base + short, :] = S[tile(k), 0:LANES].T[0:short, :]

    core_id, zi, nz = lax.rem(ti, 2), lax.div(ti, 2), n_tgt // 2
    half = height // 2
    on_src = (n_src, si, src_peers(), lambda p: (p, ti))
    on_z = (nz, zi, [lax.rem(zi + k, nz) for k in range(1, nz)], lambda p: (si, p * 2 + core_id))
    streams = [(0, half * 2 // 3, on_src, on_z, RX2a, RX3a), (half * 2 // 3, half // 3, on_z, on_src, RX2b, RX3b)]

    def span(start, size):
        return pl.ds(pl.multiple_of(start, 8), size)

    def post(source, dest, send, recv, where):
        copy = pltpu.make_async_remote_copy(
            src_ref=source, dst_ref=dest, send_sem=send, recv_sem=recv, device_id=where, device_id_type=MESH
        )
        copy.start()
        return copy

    for w, (start, size, *_) in enumerate(streams):
        theirs = span((1 - core_id) * half + start, size)
        pending.append(post(CB.at[theirs], RX1.at[start : start + size], s1.at[w], r1.at[w], mate))
    cols_wait(ITERS - 1).wait_send()
    OUT[height : height + rc, :] = (
        jnp.concatenate([f1[b] + moves[b] for b in blocks], axis=0) + SHIFT
    ) * LN2
    OUT[height + rc : height + rc + cc, :] = g * LN2

    def post_scatter(w, stage, group, base, size, RX):
        n, me, peers, where = group
        for p in peers:
            post(CB.at[span(base + p * size, size)], RX.at[me], s2.at[w, stage], r2.at[w, stage], where(p))
        return whole_wait(RX.at[pl.ds(0, n - 1)], s2.at[w, stage], r2.at[w, stage], mate)

    def post_gather(w, stage, group, base, size):
        n, me, peers, where = group
        at = span(base + me * size, size)
        for p in peers:
            post(OUT.at[at], OUT.at[at], s2.at[w, stage], r2.at[w, stage], where(p))
        return whole_wait(OUT.at[pl.ds(0, (n - 1) * size)], s2.at[w, stage], r2.at[w, stage], mate)

    def own_sum(group, base, size, RX):
        n, me, peers, where = group
        own = CB[span(base + me * size, size), :]
        for p in peers:
            own = own + RX[p]
        return own

    plans, waits = [], []
    for w, (start, size, first, second, RXa, RXb) in enumerate(streams):
        base = core_id * half + start
        block = size // first[0]
        block_at = base + first[1] * block
        piece = block // second[0]
        plans.append((base, block, block_at, piece))
        at = span(base, size)
        pending[w].wait_recv()
        CB[at, :] += RX1[start : start + size, :]
        waits.append(post_scatter(w, 0, first, base, block, RXa))
    for copy in pending:
        copy.wait_send()
    for w, (start, size, first, second, RXa, RXb) in enumerate(streams):
        base, block, block_at, piece = plans[w]
        waits[w].wait_recv()
        CB[span(block_at, block), :] = own_sum(first, base, block, RXa)
        old.append(waits[w])
        waits[w] = post_scatter(w, 1, second, block_at, piece, RXb)
    for copy in old:
        copy.wait_send()
    old = []
    for w, (start, size, first, second, RXa, RXb) in enumerate(streams):
        base, block, block_at, piece = plans[w]
        waits[w].wait_recv()
        OUT[span(block_at + second[1] * piece, piece), :] = own_sum(second, block_at, piece, RXb)
        old.append(waits[w])
        waits[w] = post_gather(w, 2, second, block_at, piece)
    for copy in old:
        copy.wait_send()
    old = []
    for w, (start, size, first, second, RXa, RXb) in enumerate(streams):
        base, block, block_at, piece = plans[w]
        waits[w].wait_recv()
        old.append(waits[w])
        waits[w] = post_gather(w, 3, first, base, block)
    for copy in old:
        copy.wait_send()
    final = []
    for w, (start, size, first, second, RXa, RXb) in enumerate(streams):
        base, block, block_at, piece = plans[w]
        waits[w].wait_recv()
        at = span(base, size)
        final.append(post(OUT.at[at], OUT.at[at], s2.at[w, 4], r2.at[w, 4], mate))
    for copy in waits:
        copy.wait_send()
    for copy in final:
        copy.wait()


def unpack(scale, dim, height, lines, f_out, g_out, core_out):
    rc, cc = f_out.shape[0], g_out.shape[0]
    f_out[...] = lines[height : height + rc, :]
    g_out[...] = lines[height + rc : height + rc + cc, :]
    full, rest = dim // LANES, dim % LANES
    line = -(-dim // 8) * 8
    short = -(-rest // 8) * 8
    for t in range(full):
        core_out[:, tile(t)] = lines[t * line : t * line + dim, :] * scale
    if rest:
        for k in range(-(-dim // LANES)):
            base = full * line + k * short
            block = jnp.concatenate(
                [lines[base : base + short, :], jnp.zeros((LANES - short, LANES), jnp.float32)], axis=0
            ).T * scale
            count = min(LANES, dim - k * LANES)
            core_out[k * LANES : k * LANES + count, full * LANES :] = block[0:count, 0:rest]


def per_device(n_src, n_tgt, src_emb_t, tgt_emb_t, core, src_logw, tgt_logw):
    dim, rows = src_emb_t.shape
    cols = tgt_emb_t.shape[1]
    f32 = jnp.float32
    line, short = -(-dim // 8) * 8, -(-(dim % LANES) // 8) * 8
    need = (dim // LANES) * line + -(-dim // LANES) * short
    nz = n_tgt // 2
    unit = 8 * n_src * nz
    half = -(-need // (6 * unit)) * 3 * unit
    height = 2 * half
    long, brief = half * 2 // 3, half // 3
    sems = pltpu.SemaphoreType.DMA
    vmem = pl.BlockSpec(memory_space=pltpu.VMEM)
    rc, cc = rows // LANES, cols // LANES
    hbm = pl.BlockSpec(memory_space=pltpu.HBM)
    lines = pl.pallas_call(
        functools.partial(kernel, n_src, n_tgt),
        out_shape=jax.ShapeDtypeStruct((height + rc + cc, LANES), f32),
        in_specs=[hbm] * 5,
        out_specs=vmem,
        scratch_shapes=[
            pltpu.VMEM(src_emb_t.shape, jnp.bfloat16),
            pltpu.VMEM(tgt_emb_t.shape, jnp.bfloat16),
            pltpu.VMEM(core.shape, f32),
            pltpu.VMEM((rc, LANES), f32),
            pltpu.VMEM((cc, LANES), f32),
            sems((5,)),
            pltpu.VMEM((rows, cols), f32),
            pltpu.VMEM((rows, dim), jnp.bfloat16),
            pltpu.VMEM((rows, LANES), f32),
            pltpu.VMEM((rows, LANES), f32),
            pltpu.VMEM((rows, LANES), f32),
            pltpu.VMEM((BLOCKS, rc // BLOCKS, LANES), f32),
            pltpu.VMEM((cc, LANES), f32),
            pltpu.VMEM((ITERS, BLOCKS, n_tgt, rc // BLOCKS, LANES), f32),
            pltpu.VMEM((ITERS, n_src, cc, LANES), f32),
            pltpu.VMEM((dim, cols), f32),
            pltpu.VMEM((height, LANES), f32),
            pltpu.VMEM((half, LANES), f32),
            pltpu.VMEM((n_src, long // n_src, LANES), f32),
            pltpu.VMEM((nz, long // (n_src * nz), LANES), f32),
            pltpu.VMEM((nz, brief // nz, LANES), f32),
            pltpu.VMEM((n_src, brief // (n_src * nz), LANES), f32),
            sems((ITERS, BLOCKS)), sems((ITERS, BLOCKS)),
            sems((ITERS,)), sems((ITERS,)),
            sems((2,)), sems((2,)),
            sems((2, 5)), sems((2, 5)),
        ],
        compiler_params=pltpu.CompilerParams(
            collective_id=0, has_side_effects=True, vmem_limit_bytes=64 * 1024 * 1024
        ),
    )(src_emb_t, tgt_emb_t, core, src_logw.reshape(rc, LANES), tgt_logw.reshape(cc, LANES))
    f, g, new = pl.pallas_call(
        functools.partial(unpack, dim / (rows * n_src), dim, height),
        out_shape=(
            jax.ShapeDtypeStruct((rc, LANES), f32),
            jax.ShapeDtypeStruct((cc, LANES), f32),
            jax.ShapeDtypeStruct((dim, dim), f32),
        ),
        in_specs=[vmem],
        out_specs=(vmem,) * 3,
        compiler_params=pltpu.CompilerParams(vmem_limit_bytes=64 * 1024 * 1024),
    )(lines)
    return f.reshape(rows), g.reshape(cols), new


def solution(mesh):
    placed = (P(None, "src"), P(None, "tgt"), P(), P("src"), P("tgt"))
    body = functools.partial(per_device, mesh.shape["src"], mesh.shape["tgt"])
    return jax.shard_map(
        body, mesh=mesh, in_specs=placed, out_specs=(P("src"), P("tgt"), P()), check_vma=False
    )
```

```python
import functools
import math

import jax
import jax.numpy as jnp
from jax import lax
from jax.experimental import pallas as pl
from jax.experimental.pallas import tpu as pltpu
from jax.sharding import PartitionSpec as P

ITERS = 3
BLOCKS = 2
LOG2E = 1.4426950408889634
LN2 = 0.6931471805599453
LANES = 128
SHIFT = 60.0
MESH = pl.DeviceIdType.MESH


def tile(t):
    return slice(t * LANES, (t + 1) * LANES)


def kernel(
    n_src, n_tgt,
    src_hbm, tgt_hbm, core_hbm, slw_hbm, tlw_hbm,
    OUT,
    src_ref, tgt_ref, core_ref, slw_ref, tlw_ref, load,
    S, proj, M, T, FB, FS, GS, RXF, RXG, W, CB, RX2a, RX3a, RX2b, RX3b,
    fsend, frecv, gsend, grecv, s2, r2,
):
    si, ti = lax.axis_index("src"), lax.axis_index("tgt")
    dim, rows = src_ref.shape
    cols = tgt_ref.shape[1]
    rc, cc = rows // LANES, cols // LANES
    f32, bf16 = jnp.float32, jnp.bfloat16

    def src_peers():
        return [lax.rem(si + k, n_src) for k in range(1, n_src)]

    def tgt_peers():
        return [lax.rem(ti + k, n_tgt) for k in range(1, n_tgt)]

    loads = [
        pltpu.make_async_copy(a, b, load.at[k])
        for k, (a, b) in enumerate(
            [(core_hbm, core_ref), (src_hbm, src_ref), (tgt_hbm, tgt_ref), (slw_hbm, slw_ref), (tlw_hbm, tlw_ref)]
        )
    ]
    for copy in loads:
        copy.start()

    mate = (si, ti + 1 - 2 * lax.rem(ti, 2))
    barrier = pltpu.get_barrier_semaphore()
    for p in src_peers():
        pl.semaphore_signal(barrier, inc=1, device_id=(p, ti), device_id_type=MESH)
        pl.semaphore_signal(barrier, inc=1, device_id=(p, mate[1]), device_id_type=MESH)
    for p in tgt_peers():
        pl.semaphore_signal(barrier, inc=1, device_id=(si, p), device_id_type=MESH)

    loads[0].wait()
    loads[1].wait()
    c32 = core_ref[...]
    c0 = c32.astype(bf16)
    c1 = (c32 - c0.astype(f32)).astype(bf16)
    src = src_ref[...]

    def contract(a, b, da, db):
        return lax.dot_general(a, b, (((da,), (db,)), ((), ())), preferred_element_type=f32)

    proj[...] = (
        contract(c0, src, 0, 0) + contract(c1, src, 0, 0)
    ).T.astype(bf16)
    for copy in loads[2:]:
        copy.wait()

    blocks = range(BLOCKS)
    tall, bc = rows // BLOCKS, rc // BLOCKS
    wide = 4 * LANES

    def groups(b, body, carry, unroll):
        def step(i, carry):
            for k in range(unroll):
                at = b * tall + (i * unroll + k) * 8
                carry = body(pl.ds(pl.multiple_of(at, 8), 8), carry)
            return carry

        return lax.fori_loop(0, tall // (8 * unroll), step, carry)

    def broadcast_down(line):
        return jnp.broadcast_to(line, (8, LANES))

    def block_tile(b, c):
        return slice(b * tall + c * LANES, b * tall + (c + 1) * LANES)

    def to_columns(b, dense):
        for c in range(bc):
            FB[block_tile(b, c), :] = jnp.broadcast_to(dense[c : c + 1, :], (LANES, LANES)).T

    def add_up(parts):
        while len(parts) > 1:
            parts = [a + b for a, b in zip(parts[::2], parts[1::2])]
        return parts[0]

    def post_all(buf, me, peers, send, recv, where):
        for p in peers:
            pltpu.make_async_remote_copy(
                src_ref=buf.at[me], dst_ref=buf.at[me], send_sem=send, recv_sem=recv,
                device_id=where(p), device_id_type=MESH,
            ).start()

    def whole_wait(ref, send, recv, where):
        return pltpu.make_async_remote_copy(
            src_ref=ref, dst_ref=ref, send_sem=send, recv_sem=recv, device_id=where, device_id_type=MESH
        )

    def post_rows(step, b):
        RXF[step, b, ti] = FS[b]
        post_all(RXF.at[step, b], ti, tgt_peers(), fsend.at[step, b], frecv.at[step, b], lambda p: (si, p))

    def rows_wait(step, b):
        ref = RXF.at[step, b, pl.ds(0, n_tgt - 1)]
        return whole_wait(ref, fsend.at[step, b], frecv.at[step, b], mate)

    def post_cols(step):
        RXG[step, si] = GS[...]
        post_all(RXG.at[step], si, src_peers(), gsend.at[step], grecv.at[step], lambda p: (p, ti))

    def cols_wait(step):
        return whole_wait(RXG.at[step, pl.ds(0, n_src - 1)], gsend.at[step], grecv.at[step], mate)

    def lse(parts):
        top = functools.reduce(jnp.maximum, parts)
        return top + jnp.log2(sum(jnp.exp2(x - top) for x in parts))

    slw = slw_ref[...] * LOG2E
    tlw = tlw_ref[...] * LOG2E

    def slw_of(b):
        return slw[b * bc : (b + 1) * bc, :]

    for b in blocks:
        mine = slice(b * tall, (b + 1) * tall)
        for t in range(cols // wide):
            at = slice(t * wide, (t + 1) * wide)
            y = jnp.dot(proj[mine, :], tgt_ref[:, at], preferred_element_type=f32) * LOG2E
            S[mine, at] = y
            top = functools.reduce(jnp.maximum, [y[:, k : k + LANES] for k in range(0, wide, LANES)])
            M[mine, :] = top if t == 0 else jnp.maximum(M[mine, :], top)

        def first_rows(r, carry):
            m = M[r, :]
            T[r, :] = add_up([jnp.exp2(S[r, tile(t)] - m) for t in range(cc)])
            return carry

        groups(b, first_rows, 0, 4)
        for c in range(bc):
            mt, st = M[block_tile(b, c), :].T, T[block_tile(b, c), :].T
            top = jnp.max(mt, axis=0, keepdims=True)
            FS[b, c : c + 1, :] = top + jnp.log2(jnp.sum(st * jnp.exp2(mt - top), axis=0, keepdims=True))
        if b == 0:
            pl.semaphore_wait(barrier, 2 * (n_src - 1) + (n_tgt - 1))
        post_rows(0, b)

    zeros = tuple(jnp.zeros((8, LANES), f32) for t in range(cc))
    f1, peaks, sums = [], [], []
    for b in blocks:
        rows_wait(0, b).wait_recv()
        f1.append(slw_of(b) - lse([RXF[0, b, k] for k in range(n_tgt)]))
        to_columns(b, f1[b])

        def peak_cols(r, acc):
            fb = FB[r, :]
            return tuple(jnp.maximum(a, S[r, tile(t)] + fb) for t, a in enumerate(acc))

        acc = groups(b, peak_cols, tuple(jnp.full((8, LANES), -jnp.inf, f32) for t in range(cc)), 4)
        for t in range(cc):
            GS[t : t + 1, :] = jnp.max(acc[t], axis=0, keepdims=True)
        peaks.append(GS[...])
        less = [broadcast_down(SHIFT - peaks[b][t : t + 1, :]) for t in range(cc)]

        def first_cols(r, acc):
            fb = FB[r, :]
            new = []
            for t, a in enumerate(acc):
                e = jnp.exp2(S[r, tile(t)] + fb + less[t])
                S[r, tile(t)] = e
                new.append(a + e)
            return tuple(new)

        acc = groups(b, first_cols, zeros, 2)
        for t in range(cc):
            GS[t : t + 1, :] = jnp.sum(acc[t], axis=0, keepdims=True)
        sums.append(peaks[b] + (jnp.log2(GS[...]) - SHIFT))
    GS[...] = lse(sums)
    post_cols(0)
    for b in blocks:
        rows_wait(0, b).wait_send()
    cols_wait(0).wait_recv()
    g = tlw - lse([RXG[0, k] for k in range(n_src)])
    v = [jnp.exp2(peaks[b] + g) for b in blocks]

    for step in range(1, ITERS):
        last = step == ITERS - 1
        for b in blocks:
            vb = [broadcast_down(v[b][t : t + 1, :]) for t in range(cc)]

            def later_rows(r, carry):
                T[r, :] = add_up([S[r, tile(t)] * vb[t] for t in range(cc)])
                return carry

            groups(b, later_rows, 0, 4)
            for c in range(bc):
                FS[b, c : c + 1, :] = jnp.sum(T[block_tile(b, c), :].T, axis=0, keepdims=True)
            post_rows(step, b)
        cols_wait(step - 1).wait_send()
        moves, sums = [], []
        for b in blocks:
            rows_wait(step, b).wait_recv()
            moves.append(slw_of(b) - jnp.log2(sum(RXF[step, b, k] for k in range(n_tgt))))
            to_columns(b, jnp.exp2(moves[b]))

            def later_cols(r, acc):
                ub = FB[r, :]
                new = []
                for t, a in enumerate(acc):
                    e = S[r, tile(t)] * ub
                    if last:
                        S[r, tile(t)] = e
                    new.append(a + e)
                return tuple(new)

            acc = groups(b, later_cols, zeros, 4)
            for t in range(cc):
                GS[t : t + 1, :] = jnp.sum(acc[t], axis=0, keepdims=True)
            sums.append(GS[...] * v[b])
        GS[...] = sum(sums)
        post_cols(step)
        for b in blocks:
            rows_wait(step, b).wait_send()
        if last:
            peak = functools.reduce(jnp.maximum, peaks)
            ratio = [jnp.exp2(peaks[b] - peak) for b in blocks]
            for t in range(0, cc, 2):
                at = slice(t * LANES, (t + 2) * LANES)
                whole = jnp.concatenate(
                    [
                        jnp.concatenate(
                            [
                                (S[b * tall : (b + 1) * tall, tile(k)] * ratio[b][k : k + 1, :]).astype(bf16)
                                for b in blocks
                            ],
                            axis=0,
                        )
                        for k in (t, t + 1)
                    ],
                    axis=1,
                )
                W[:, at] = jnp.dot(src_ref[...], whole, preferred_element_type=f32)
        cols_wait(step).wait_recv()
        g = g + (tlw - jnp.log2(sum(RXG[step, k] for k in range(n_src))))
        if not last:
            v = [jnp.exp2(peaks[b] + g) for b in blocks]

    end = jnp.exp2(peak + g)
    total = None
    for t in range(0, cc, 4):
        at = slice(t * LANES, (t + 4) * LANES)
        x = jnp.concatenate([W[:, tile(k)] * end[k : k + 1, :] for k in range(t, t + 4)], axis=1)
        part = contract(x.astype(bf16), tgt_ref[:, at], 1, 1)
        total = part if total is None else total + part

    height = CB.shape[0]
    full, rest = dim // LANES, dim % LANES
    line = -(-dim // 8) * 8
    short = -(-rest // 8) * 8
    CB[...] = jnp.zeros(CB.shape, f32)
    for t in range(full):
        CB[t * line : t * line + dim, :] = total[:, tile(t)]
    if rest:
        plan_rows = -(-dim // LANES) * LANES
        S[0:plan_rows, 0:LANES] = jnp.zeros((plan_rows, LANES), f32)
        S[0:dim, 0:rest] = total[:, full * LANES :]
        for k in range(plan_rows // LANES):
            base = full * line + k * short
            CB[base : base + short, :] = S[tile(k), 0:LANES].T[0:short, :]

    core_id, zi, nz = lax.rem(ti, 2), lax.div(ti, 2), n_tgt // 2
    on_src = [(p, m) for p in [si] + src_peers() for m in (ti, mate[1])][1:]
    on_z = [(si, p) for p in tgt_peers()]
    over_src = [(p, ti) for p in src_peers()]
    over_z = [(si, lax.rem(zi + k, nz) * 2 + core_id) for k in range(1, nz)]

    def by_plane(d):
        return d[0] * 2 + lax.rem(d[1], 2)

    def by_column(d):
        return d[1]

    long = height * 2 // 3
    streams = [
        (0, long // (2 * n_src), 2 * n_src, on_src, by_plane, nz, over_z, zi, RX2a, RX3a),
        (long, (height - long) // n_tgt, n_tgt, on_z, by_column, n_src, over_src, si, RX2b, RX3b),
    ]

    def span(start, size):
        return pl.ds(pl.multiple_of(start, 8), size)

    def post(source, dest, send, recv, where):
        pltpu.make_async_remote_copy(
            src_ref=source, dst_ref=dest, send_sem=send, recv_sem=recv, device_id=where, device_id_type=MESH
        ).start()

    waits, old = [], [cols_wait(ITERS - 1)]
    for w, (start, size, n, peers, index, n2, peers2, me2, RXa, RXb) in enumerate(streams):
        me = index((si, ti))
        for d in peers:
            at = span(start + index(d) * size, size)
            post(CB.at[at], RXa.at[me], s2.at[w, 0], r2.at[w, 0], d)
        waits.append(whole_wait(RXa.at[pl.ds(0, n - 1)], s2.at[w, 0], r2.at[w, 0], mate))
    OUT[height : height + rc, :] = (
        jnp.concatenate([f1[b] + moves[b] for b in blocks], axis=0) + SHIFT
    ) * LN2
    OUT[height + rc : height + rc + cc, :] = g * LN2
    for wait in old:
        wait.wait_send()
    old = []
    for w, (start, size, n, peers, index, n2, peers2, me2, RXa, RXb) in enumerate(streams):
        own = CB[span(start + index((si, ti)) * size, size), :]
        waits[w].wait_recv()
        for d in peers:
            own = own + RXa[index(d)]
        RXb[me2] = own
        for d in peers2:
            post(RXb.at[me2], RXb.at[me2], s2.at[w, 1], r2.at[w, 1], d)
        old.append(waits[w])
        waits[w] = whole_wait(RXb.at[pl.ds(0, n2 - 1)], s2.at[w, 1], r2.at[w, 1], mate)
    for wait in old:
        wait.wait_send()
    old = []
    for w, (start, size, n, peers, index, n2, peers2, me2, RXa, RXb) in enumerate(streams):
        waits[w].wait_recv()
        at = span(start + index((si, ti)) * size, size)
        OUT[at, :] = sum(RXb[k] for k in range(n2))
        for d in peers:
            post(OUT.at[at], OUT.at[at], s2.at[w, 2], r2.at[w, 2], d)
        old.append(waits[w])
        waits[w] = whole_wait(OUT.at[pl.ds(0, (n - 1) * size)], s2.at[w, 2], r2.at[w, 2], mate)
    for wait in old:
        wait.wait_send()
    for wait in waits:
        wait.wait()


def unpack(scale, dim, height, lines, f_out, g_out, core_out):
    rc, cc = f_out.shape[0], g_out.shape[0]
    f_out[...] = lines[height : height + rc, :]
    g_out[...] = lines[height + rc : height + rc + cc, :]
    full, rest = dim // LANES, dim % LANES
    line = -(-dim // 8) * 8
    short = -(-rest // 8) * 8
    for t in range(full):
        core_out[:, tile(t)] = lines[t * line : t * line + dim, :] * scale
    if rest:
        for k in range(-(-dim // LANES)):
            base = full * line + k * short
            block = jnp.concatenate(
                [lines[base : base + short, :], jnp.zeros((LANES - short, LANES), jnp.float32)], axis=0
            ).T * scale
            count = min(LANES, dim - k * LANES)
            core_out[k * LANES : k * LANES + count, full * LANES :] = block[0:count, 0:rest]


def per_device(n_src, n_tgt, src_emb_t, tgt_emb_t, core, src_logw, tgt_logw):
    dim, rows = src_emb_t.shape
    cols = tgt_emb_t.shape[1]
    f32 = jnp.float32
    line, short = -(-dim // 8) * 8, -(-(dim % LANES) // 8) * 8
    need = (dim // LANES) * line + -(-dim // LANES) * short
    nz = n_tgt // 2
    unit = 16 * math.lcm(n_src, nz)
    height = -(-need // (3 * unit)) * 3 * unit
    long = height * 2 // 3
    block, brief = long // (2 * n_src), (height - long) // n_tgt
    sems = pltpu.SemaphoreType.DMA
    vmem = pl.BlockSpec(memory_space=pltpu.VMEM)
    rc, cc = rows // LANES, cols // LANES
    hbm = pl.BlockSpec(memory_space=pltpu.HBM)
    lines = pl.pallas_call(
        functools.partial(kernel, n_src, n_tgt),
        out_shape=jax.ShapeDtypeStruct((height + rc + cc, LANES), f32),
        in_specs=[hbm] * 5,
        out_specs=vmem,
        scratch_shapes=[
            pltpu.VMEM(src_emb_t.shape, jnp.bfloat16),
            pltpu.VMEM(tgt_emb_t.shape, jnp.bfloat16),
            pltpu.VMEM(core.shape, f32),
            pltpu.VMEM((rc, LANES), f32),
            pltpu.VMEM((cc, LANES), f32),
            sems((5,)),
            pltpu.VMEM((rows, cols), f32),
            pltpu.VMEM((rows, dim), jnp.bfloat16),
            pltpu.VMEM((rows, LANES), f32),
            pltpu.VMEM((rows, LANES), f32),
            pltpu.VMEM((rows, LANES), f32),
            pltpu.VMEM((BLOCKS, rc // BLOCKS, LANES), f32),
            pltpu.VMEM((cc, LANES), f32),
            pltpu.VMEM((ITERS, BLOCKS, n_tgt, rc // BLOCKS, LANES), f32),
            pltpu.VMEM((ITERS, n_src, cc, LANES), f32),
            pltpu.VMEM((dim, cols), f32),
            pltpu.VMEM((height, LANES), f32),
            pltpu.VMEM((2 * n_src, block, LANES), f32),
            pltpu.VMEM((nz, block, LANES), f32),
            pltpu.VMEM((n_tgt, brief, LANES), f32),
            pltpu.VMEM((n_src, brief, LANES), f32),
            sems((ITERS, BLOCKS)), sems((ITERS, BLOCKS)),
            sems((ITERS,)), sems((ITERS,)),
            sems((2, 3)), sems((2, 3)),
        ],
        compiler_params=pltpu.CompilerParams(
            collective_id=0, has_side_effects=True, vmem_limit_bytes=64 * 1024 * 1024
        ),
    )(src_emb_t, tgt_emb_t, core, src_logw.reshape(rc, LANES), tgt_logw.reshape(cc, LANES))
    f, g, new = pl.pallas_call(
        functools.partial(unpack, dim / (rows * n_src), dim, height),
        out_shape=(
            jax.ShapeDtypeStruct((rc, LANES), f32),
            jax.ShapeDtypeStruct((cc, LANES), f32),
            jax.ShapeDtypeStruct((dim, dim), f32),
        ),
        in_specs=[vmem],
        out_specs=(vmem,) * 3,
        compiler_params=pltpu.CompilerParams(vmem_limit_bytes=64 * 1024 * 1024),
    )(lines)
    return f.reshape(rows), g.reshape(cols), new


def solution(mesh):
    placed = (P(None, "src"), P(None, "tgt"), P(), P("src"), P("tgt"))
    body = functools.partial(per_device, mesh.shape["src"], mesh.shape["tgt"])
    return jax.shard_map(
        body, mesh=mesh, in_specs=placed, out_specs=(P("src"), P("tgt"), P()), check_vma=False
    )
```

```python
import functools
import math

import jax
import jax.numpy as jnp
from jax import lax
from jax.experimental import pallas as pl
from jax.experimental.pallas import tpu as pltpu
from jax.sharding import PartitionSpec as P

ITERS = 3
BLOCKS = 2
LOG2E = 1.4426950408889634
LN2 = 0.6931471805599453
LANES = 128
SHIFT = 60.0
MESH = pl.DeviceIdType.MESH


def tile(t):
    return slice(t * LANES, (t + 1) * LANES)


def kernel(
    n_src, n_tgt,
    src_hbm, tgt_hbm, core_hbm, slw_hbm, tlw_hbm,
    OUT,
    src_ref, tgt_ref, core_ref, slw_ref, tlw_ref, load,
    S, proj, M, T, FB, FS, GS, RXF, RXG, W, CB, RX2a, RX3a, RX2b, RX3b,
    fsend, frecv, gsend, grecv, s2, r2,
):
    si, ti = lax.axis_index("src"), lax.axis_index("tgt")
    dim, rows = src_ref.shape
    cols = tgt_ref.shape[1]
    rc, cc = rows // LANES, cols // LANES
    f32, bf16 = jnp.float32, jnp.bfloat16

    def src_peers():
        return [lax.rem(si + k, n_src) for k in range(1, n_src)]

    def tgt_peers():
        order = sorted(range(1, n_tgt), key=lambda k: abs(k - n_tgt // 2))
        return [lax.rem(ti + k, n_tgt) for k in order]

    loads = [
        pltpu.make_async_copy(a, b, load.at[k])
        for k, (a, b) in enumerate(
            [(core_hbm, core_ref), (src_hbm, src_ref), (tgt_hbm, tgt_ref), (slw_hbm, slw_ref), (tlw_hbm, tlw_ref)]
        )
    ]
    for copy in loads:
        copy.start()

    mate = (si, ti + 1 - 2 * lax.rem(ti, 2))
    barrier = pltpu.get_barrier_semaphore()
    for p in src_peers():
        pl.semaphore_signal(barrier, inc=1, device_id=(p, ti), device_id_type=MESH)
        pl.semaphore_signal(barrier, inc=1, device_id=(p, mate[1]), device_id_type=MESH)
    for p in tgt_peers():
        pl.semaphore_signal(barrier, inc=1, device_id=(si, p), device_id_type=MESH)

    loads[0].wait()
    loads[1].wait()
    c32 = core_ref[...]
    c0 = c32.astype(bf16)
    c1 = (c32 - c0.astype(f32)).astype(bf16)
    src = src_ref[...]

    def contract(a, b, da, db):
        return lax.dot_general(a, b, (((da,), (db,)), ((), ())), preferred_element_type=f32)

    proj[...] = (
        contract(c0, src, 0, 0) + contract(c1, src, 0, 0)
    ).T.astype(bf16)
    for copy in loads[2:]:
        copy.wait()

    blocks = range(BLOCKS)
    tall, bc = rows // BLOCKS, rc // BLOCKS
    wide = 4 * LANES

    def groups(b, body, carry, unroll):
        def step(i, carry):
            for k in range(unroll):
                at = b * tall + (i * unroll + k) * 8
                carry = body(pl.ds(pl.multiple_of(at, 8), 8), carry)
            return carry

        return lax.fori_loop(0, tall // (8 * unroll), step, carry)

    def broadcast_down(line):
        return jnp.broadcast_to(line, (8, LANES))

    def block_tile(b, c):
        return slice(b * tall + c * LANES, b * tall + (c + 1) * LANES)

    def to_columns(b, dense):
        for c in range(bc):
            FB[block_tile(b, c), :] = jnp.broadcast_to(dense[c : c + 1, :], (LANES, LANES)).T

    def add_up(parts):
        while len(parts) > 1:
            parts = [a + b for a, b in zip(parts[::2], parts[1::2])]
        return parts[0]

    def post_all(buf, me, peers, send, recv, where):
        for p in peers:
            pltpu.make_async_remote_copy(
                src_ref=buf.at[me], dst_ref=buf.at[me], send_sem=send, recv_sem=recv,
                device_id=where(p), device_id_type=MESH,
            ).start()

    def whole_wait(ref, send, recv, where):
        return pltpu.make_async_remote_copy(
            src_ref=ref, dst_ref=ref, send_sem=send, recv_sem=recv, device_id=where, device_id_type=MESH
        )

    def post_rows(step, b):
        RXF[step, b, ti] = FS[b]
        post_all(RXF.at[step, b], ti, tgt_peers(), fsend.at[step, b], frecv.at[step, b], lambda p: (si, p))

    def rows_wait(step, b):
        ref = RXF.at[step, b, pl.ds(0, n_tgt - 1)]
        return whole_wait(ref, fsend.at[step, b], frecv.at[step, b], mate)

    def post_cols(step):
        RXG[step, si] = GS[...]
        post_all(RXG.at[step], si, src_peers(), gsend.at[step], grecv.at[step], lambda p: (p, ti))

    def cols_wait(step):
        return whole_wait(RXG.at[step, pl.ds(0, n_src - 1)], gsend.at[step], grecv.at[step], mate)

    def lse(parts):
        top = functools.reduce(jnp.maximum, parts)
        return top + jnp.log2(sum(jnp.exp2(x - top) for x in parts))

    slw = slw_ref[...] * LOG2E
    tlw = tlw_ref[...] * LOG2E

    def slw_of(b):
        return slw[b * bc : (b + 1) * bc, :]

    for b in blocks:
        mine = slice(b * tall, (b + 1) * tall)
        for t in range(cols // wide):
            at = slice(t * wide, (t + 1) * wide)
            y = jnp.dot(proj[mine, :], tgt_ref[:, at], preferred_element_type=f32) * LOG2E
            S[mine, at] = y
            top = functools.reduce(jnp.maximum, [y[:, k : k + LANES] for k in range(0, wide, LANES)])
            M[mine, :] = top if t == 0 else jnp.maximum(M[mine, :], top)

        def first_rows(r, carry):
            m = M[r, :]
            T[r, :] = add_up([jnp.exp2(S[r, tile(t)] - m) for t in range(cc)])
            return carry

        groups(b, first_rows, 0, 4)
        for c in range(bc):
            mt, st = M[block_tile(b, c), :].T, T[block_tile(b, c), :].T
            top = jnp.max(mt, axis=0, keepdims=True)
            FS[b, c : c + 1, :] = top + jnp.log2(jnp.sum(st * jnp.exp2(mt - top), axis=0, keepdims=True))
        if b == 0:
            pl.semaphore_wait(barrier, 2 * (n_src - 1) + (n_tgt - 1))
        post_rows(0, b)

    zeros = tuple(jnp.zeros((8, LANES), f32) for t in range(cc))
    f1, peaks, sums = [], [], []
    for b in blocks:
        rows_wait(0, b).wait_recv()
        f1.append(slw_of(b) - lse([RXF[0, b, k] for k in range(n_tgt)]))
        to_columns(b, f1[b])

        def peak_cols(r, acc):
            fb = FB[r, :]
            return tuple(jnp.maximum(a, S[r, tile(t)] + fb) for t, a in enumerate(acc))

        acc = groups(b, peak_cols, tuple(jnp.full((8, LANES), -jnp.inf, f32) for t in range(cc)), 4)
        for t in range(cc):
            GS[t : t + 1, :] = jnp.max(acc[t], axis=0, keepdims=True)
        peaks.append(GS[...])
        less = [broadcast_down(SHIFT - peaks[b][t : t + 1, :]) for t in range(cc)]

        def first_cols(r, acc):
            fb = FB[r, :]
            new = []
            for t, a in enumerate(acc):
                e = jnp.exp2(S[r, tile(t)] + fb + less[t])
                S[r, tile(t)] = e
                new.append(a + e)
            return tuple(new)

        acc = groups(b, first_cols, zeros, 2)
        for t in range(cc):
            GS[t : t + 1, :] = jnp.sum(acc[t], axis=0, keepdims=True)
        sums.append(peaks[b] + (jnp.log2(GS[...]) - SHIFT))
    GS[...] = lse(sums)
    post_cols(0)
    for b in blocks:
        rows_wait(0, b).wait_send()
    cols_wait(0).wait_recv()
    g = tlw - lse([RXG[0, k] for k in range(n_src)])
    v = [jnp.exp2(peaks[b] + g) for b in blocks]

    for step in range(1, ITERS):
        last = step == ITERS - 1
        for b in blocks:
            vb = [broadcast_down(v[b][t : t + 1, :]) for t in range(cc)]

            def later_rows(r, carry):
                T[r, :] = add_up([S[r, tile(t)] * vb[t] for t in range(cc)])
                return carry

            groups(b, later_rows, 0, 4)
            for c in range(bc):
                FS[b, c : c + 1, :] = jnp.sum(T[block_tile(b, c), :].T, axis=0, keepdims=True)
            post_rows(step, b)
        cols_wait(step - 1).wait_send()
        moves, sums = [], []
        for b in blocks:
            rows_wait(step, b).wait_recv()
            moves.append(slw_of(b) - jnp.log2(sum(RXF[step, b, k] for k in range(n_tgt))))
            to_columns(b, jnp.exp2(moves[b]))

            def later_cols(r, acc):
                ub = FB[r, :]
                new = []
                for t, a in enumerate(acc):
                    e = S[r, tile(t)] * ub
                    if last:
                        S[r, tile(t)] = e
                    new.append(a + e)
                return tuple(new)

            acc = groups(b, later_cols, zeros, 4)
            for t in range(cc):
                GS[t : t + 1, :] = jnp.sum(acc[t], axis=0, keepdims=True)
            sums.append(GS[...] * v[b])
        GS[...] = sum(sums)
        post_cols(step)
        for b in blocks:
            rows_wait(step, b).wait_send()
        if last:
            CB[...] = jnp.zeros(CB.shape, f32)
            peak = functools.reduce(jnp.maximum, peaks)
            ratio = [jnp.exp2(peaks[b] - peak) for b in blocks]
            for t in range(0, cc, 2):
                at = slice(t * LANES, (t + 2) * LANES)
                whole = jnp.concatenate(
                    [
                        jnp.concatenate(
                            [
                                (S[b * tall : (b + 1) * tall, tile(k)] * ratio[b][k : k + 1, :]).astype(bf16)
                                for b in blocks
                            ],
                            axis=0,
                        )
                        for k in (t, t + 1)
                    ],
                    axis=1,
                )
                W[:, at] = jnp.dot(src_ref[...], whole, preferred_element_type=f32)
        cols_wait(step).wait_recv()
        g = g + (tlw - jnp.log2(sum(RXG[step, k] for k in range(n_src))))
        if not last:
            v = [jnp.exp2(peaks[b] + g) for b in blocks]

    height = CB.shape[0]
    core_id, zi, nz = lax.rem(ti, 2), lax.div(ti, 2), n_tgt // 2
    on_src = [(p, m) for p in src_peers() for m in (ti, mate[1])] + [mate]
    on_z = [(si, p) for p in tgt_peers()]
    over_src = [(p, ti) for p in src_peers()]
    over_z = [(si, lax.rem(zi + k, nz) * 2 + core_id) for k in range(1, nz)]

    def by_plane(d):
        return d[0] * 2 + lax.rem(d[1], 2)

    def by_column(d):
        return d[1]

    long = height * 2 // 3
    streams = [
        (0, long // (2 * n_src), 2 * n_src, on_src, by_plane, nz, over_z, zi, RX2a, RX3a),
        (long, (height - long) // n_tgt, n_tgt, on_z, by_column, n_src, over_src, si, RX2b, RX3b),
    ]

    def span(start, size):
        return pl.ds(pl.multiple_of(start, 8), size)

    def post(source, dest, send, recv, where):
        pltpu.make_async_remote_copy(
            src_ref=source, dst_ref=dest, send_sem=send, recv_sem=recv, device_id=where, device_id_type=MESH
        ).start()

    waits, old = [None, None], [cols_wait(ITERS - 1)]

    def scatter(w):
        start, size, n, peers, index, n2, peers2, me2, RXa, RXb = streams[w]
        me = index((si, ti))
        for d in peers:
            at = span(start + index(d) * size, size)
            post(CB.at[at], RXa.at[me], s2.at[w, 0], r2.at[w, 0], d)
        waits[w] = whole_wait(RXa.at[pl.ds(0, n - 1)], s2.at[w, 0], r2.at[w, 0], mate)

    end = jnp.exp2(peak + g)
    step = 4
    weighed = [
        jnp.concatenate([W[:, tile(k)] * end[k : k + 1, :] for k in range(t, t + step)], axis=1).astype(bf16)
        for t in range(0, cc, step)
    ]

    def product(low, high):
        return sum(
            contract(x, tgt_ref[low:high, k * step * LANES : (k + 1) * step * LANES], 1, 1)
            for k, x in enumerate(weighed)
        )

    full, rest = dim // LANES, dim % LANES
    line = -(-dim // 8) * 8
    short = -(-rest // 8) * 8
    right = product(LANES, dim)
    for t in range(1, full):
        CB[t * line : t * line + dim, :] = right[:, tile(t - 1)]
    if rest:
        plan_rows = -(-dim // LANES) * LANES
        S[0:plan_rows, 0:LANES] = jnp.zeros((plan_rows, LANES), f32)
        S[0:dim, 0:rest] = right[:, (full - 1) * LANES :]
        for k in range(plan_rows // LANES):
            base = full * line + k * short
            CB[base : base + short, :] = S[tile(k), 0:LANES].T[0:short, :]
    scatter(1)
    CB[0:dim, :] = product(0, LANES)
    scatter(0)
    OUT[height : height + rc, :] = (
        jnp.concatenate([f1[b] + moves[b] for b in blocks], axis=0) + SHIFT
    ) * LN2
    OUT[height + rc : height + rc + cc, :] = g * LN2
    for wait in old:
        wait.wait_send()
    old = []
    for w, (start, size, n, peers, index, n2, peers2, me2, RXa, RXb) in enumerate(streams):
        own = CB[span(start + index((si, ti)) * size, size), :]
        waits[w].wait_recv()
        for d in peers:
            own = own + RXa[index(d)]
        RXb[me2] = own
        for d in peers2:
            post(RXb.at[me2], RXb.at[me2], s2.at[w, 1], r2.at[w, 1], d)
        old.append(waits[w])
        waits[w] = whole_wait(RXb.at[pl.ds(0, n2 - 1)], s2.at[w, 1], r2.at[w, 1], mate)
    for wait in old:
        wait.wait_send()
    old = []
    for w, (start, size, n, peers, index, n2, peers2, me2, RXa, RXb) in enumerate(streams):
        waits[w].wait_recv()
        at = span(start + index((si, ti)) * size, size)
        OUT[at, :] = sum(RXb[k] for k in range(n2))
        for d in peers:
            post(OUT.at[at], OUT.at[at], s2.at[w, 2], r2.at[w, 2], d)
        old.append(waits[w])
        waits[w] = whole_wait(OUT.at[pl.ds(0, (n - 1) * size)], s2.at[w, 2], r2.at[w, 2], mate)
    for wait in old:
        wait.wait_send()
    for wait in waits:
        wait.wait()


def unpack(scale, dim, height, lines, f_out, g_out, core_out):
    rc, cc = f_out.shape[0], g_out.shape[0]
    f_out[...] = lines[height : height + rc, :]
    g_out[...] = lines[height + rc : height + rc + cc, :]
    full, rest = dim // LANES, dim % LANES
    line = -(-dim // 8) * 8
    short = -(-rest // 8) * 8
    for t in range(full):
        core_out[:, tile(t)] = lines[t * line : t * line + dim, :] * scale
    if rest:
        for k in range(-(-dim // LANES)):
            base = full * line + k * short
            block = jnp.concatenate(
                [lines[base : base + short, :], jnp.zeros((LANES - short, LANES), jnp.float32)], axis=0
            ).T * scale
            count = min(LANES, dim - k * LANES)
            core_out[k * LANES : k * LANES + count, full * LANES :] = block[0:count, 0:rest]


def per_device(n_src, n_tgt, src_emb_t, tgt_emb_t, core, src_logw, tgt_logw):
    dim, rows = src_emb_t.shape
    cols = tgt_emb_t.shape[1]
    f32 = jnp.float32
    line, short = -(-dim // 8) * 8, -(-(dim % LANES) // 8) * 8
    need = (dim // LANES) * line + -(-dim // LANES) * short
    nz = n_tgt // 2
    unit = 16 * math.lcm(n_src, nz)
    height = -(-need // (3 * unit)) * 3 * unit
    long = height * 2 // 3
    block, brief = long // (2 * n_src), (height - long) // n_tgt
    sems = pltpu.SemaphoreType.DMA
    vmem = pl.BlockSpec(memory_space=pltpu.VMEM)
    rc, cc = rows // LANES, cols // LANES
    hbm = pl.BlockSpec(memory_space=pltpu.HBM)
    lines = pl.pallas_call(
        functools.partial(kernel, n_src, n_tgt),
        out_shape=jax.ShapeDtypeStruct((height + rc + cc, LANES), f32),
        in_specs=[hbm] * 5,
        out_specs=vmem,
        scratch_shapes=[
            pltpu.VMEM(src_emb_t.shape, jnp.bfloat16),
            pltpu.VMEM(tgt_emb_t.shape, jnp.bfloat16),
            pltpu.VMEM(core.shape, f32),
            pltpu.VMEM((rc, LANES), f32),
            pltpu.VMEM((cc, LANES), f32),
            sems((5,)),
            pltpu.VMEM((rows, cols), f32),
            pltpu.VMEM((rows, dim), jnp.bfloat16),
            pltpu.VMEM((rows, LANES), f32),
            pltpu.VMEM((rows, LANES), f32),
            pltpu.VMEM((rows, LANES), f32),
            pltpu.VMEM((BLOCKS, rc // BLOCKS, LANES), f32),
            pltpu.VMEM((cc, LANES), f32),
            pltpu.VMEM((ITERS, BLOCKS, n_tgt, rc // BLOCKS, LANES), f32),
            pltpu.VMEM((ITERS, n_src, cc, LANES), f32),
            pltpu.VMEM((dim, cols), f32),
            pltpu.VMEM((height, LANES), f32),
            pltpu.VMEM((2 * n_src, block, LANES), f32),
            pltpu.VMEM((nz, block, LANES), f32),
            pltpu.VMEM((n_tgt, brief, LANES), f32),
            pltpu.VMEM((n_src, brief, LANES), f32),
            sems((ITERS, BLOCKS)), sems((ITERS, BLOCKS)),
            sems((ITERS,)), sems((ITERS,)),
            sems((2, 3)), sems((2, 3)),
        ],
        compiler_params=pltpu.CompilerParams(
            collective_id=0, has_side_effects=True, vmem_limit_bytes=64 * 1024 * 1024
        ),
    )(src_emb_t, tgt_emb_t, core, src_logw.reshape(rc, LANES), tgt_logw.reshape(cc, LANES))
    f, g, new = pl.pallas_call(
        functools.partial(unpack, dim / (rows * n_src), dim, height),
        out_shape=(
            jax.ShapeDtypeStruct((rc, LANES), f32),
            jax.ShapeDtypeStruct((cc, LANES), f32),
            jax.ShapeDtypeStruct((dim, dim), f32),
        ),
        in_specs=[vmem],
        out_specs=(vmem,) * 3,
        compiler_params=pltpu.CompilerParams(vmem_limit_bytes=64 * 1024 * 1024),
    )(lines)
    return f.reshape(rows), g.reshape(cols), new


def solution(mesh):
    placed = (P(None, "src"), P(None, "tgt"), P(), P("src"), P("tgt"))
    body = functools.partial(per_device, mesh.shape["src"], mesh.shape["tgt"])
    return jax.shard_map(
        body, mesh=mesh, in_specs=placed, out_specs=(P("src"), P("tgt"), P()), check_vma=False
    )
```

```python
import functools
import math

import jax
import jax.numpy as jnp
from jax import lax
from jax.experimental import pallas as pl
from jax.experimental.pallas import tpu as pltpu
from jax.sharding import PartitionSpec as P

ITERS = 3
BLOCKS = 2
LOG2E = 1.4426950408889634
LN2 = 0.6931471805599453
LANES = 128
SHIFT = 60.0
MESH = pl.DeviceIdType.MESH


def tile(t):
    return slice(t * LANES, (t + 1) * LANES)


def kernel(
    n_src, n_tgt,
    src_hbm, tgt_hbm, core_hbm, slw_hbm, tlw_hbm,
    OUT,
    src_ref, tgt_ref, core_ref, slw_ref, tlw_ref, load,
    S, proj, M, T, FB, FS, GS, RXF, RXG, W, CB, RX2a, RX3a, RX2b, RX3b,
    fsend, frecv, gsend, grecv, s2, r2,
):
    si, ti = lax.axis_index("src"), lax.axis_index("tgt")
    dim, rows = src_ref.shape
    cols = tgt_ref.shape[1]
    rc, cc = rows // LANES, cols // LANES
    f32, bf16 = jnp.float32, jnp.bfloat16

    def src_peers():
        return [lax.rem(si + k, n_src) for k in range(1, n_src)]

    def tgt_peers():
        order = sorted(range(1, n_tgt), key=lambda k: abs(k - n_tgt // 2))
        return [lax.rem(ti + k, n_tgt) for k in order]

    loads = [
        pltpu.make_async_copy(a, b, load.at[k])
        for k, (a, b) in enumerate(
            [(core_hbm, core_ref), (src_hbm, src_ref), (tgt_hbm, tgt_ref), (slw_hbm, slw_ref), (tlw_hbm, tlw_ref)]
        )
    ]
    for copy in loads:
        copy.start()

    mate = (si, ti + 1 - 2 * lax.rem(ti, 2))
    barrier = pltpu.get_barrier_semaphore()
    for p in src_peers():
        pl.semaphore_signal(barrier, inc=1, device_id=(p, ti), device_id_type=MESH)
        pl.semaphore_signal(barrier, inc=1, device_id=(p, mate[1]), device_id_type=MESH)
    for p in tgt_peers():
        pl.semaphore_signal(barrier, inc=1, device_id=(si, p), device_id_type=MESH)

    loads[0].wait()
    loads[1].wait()
    c32 = core_ref[...]
    c0 = c32.astype(bf16)
    c1 = (c32 - c0.astype(f32)).astype(bf16)
    src = src_ref[...]

    def contract(a, b, da, db):
        return lax.dot_general(a, b, (((da,), (db,)), ((), ())), preferred_element_type=f32)

    proj[...] = (
        contract(c0, src, 0, 0) + contract(c1, src, 0, 0)
    ).T.astype(bf16)
    for copy in loads[2:]:
        copy.wait()

    blocks = range(BLOCKS)
    tall, bc = rows // BLOCKS, rc // BLOCKS
    wide = 4 * LANES

    def groups(b, body, carry, unroll):
        def step(i, carry):
            for k in range(unroll):
                at = b * tall + (i * unroll + k) * 8
                carry = body(pl.ds(pl.multiple_of(at, 8), 8), carry)
            return carry

        return lax.fori_loop(0, tall // (8 * unroll), step, carry)

    def broadcast_down(line):
        return jnp.broadcast_to(line, (8, LANES))

    def block_tile(b, c):
        return slice(b * tall + c * LANES, b * tall + (c + 1) * LANES)

    def to_columns(b, dense):
        for c in range(bc):
            FB[block_tile(b, c), :] = jnp.broadcast_to(dense[c : c + 1, :], (LANES, LANES)).T

    def add_up(parts):
        while len(parts) > 1:
            parts = [a + b for a, b in zip(parts[::2], parts[1::2])]
        return parts[0]

    def post_all(buf, me, peers, send, recv, where):
        for p in peers:
            pltpu.make_async_remote_copy(
                src_ref=buf.at[me], dst_ref=buf.at[me], send_sem=send, recv_sem=recv,
                device_id=where(p), device_id_type=MESH,
            ).start()

    def whole_wait(ref, send, recv, where):
        return pltpu.make_async_remote_copy(
            src_ref=ref, dst_ref=ref, send_sem=send, recv_sem=recv, device_id=where, device_id_type=MESH
        )

    def post_rows(step, b):
        RXF[step, b, ti] = FS[b]
        post_all(RXF.at[step, b], ti, tgt_peers(), fsend.at[step, b], frecv.at[step, b], lambda p: (si, p))

    def rows_wait(step, b):
        ref = RXF.at[step, b, pl.ds(0, n_tgt - 1)]
        return whole_wait(ref, fsend.at[step, b], frecv.at[step, b], mate)

    def post_cols(step):
        RXG[step, si] = GS[...]
        post_all(RXG.at[step], si, src_peers(), gsend.at[step], grecv.at[step], lambda p: (p, ti))

    def cols_wait(step):
        return whole_wait(RXG.at[step, pl.ds(0, n_src - 1)], gsend.at[step], grecv.at[step], mate)

    def lse(parts):
        top = functools.reduce(jnp.maximum, parts)
        return top + jnp.log2(sum(jnp.exp2(x - top) for x in parts))

    slw = slw_ref[...] * LOG2E
    tlw = tlw_ref[...] * LOG2E

    def slw_of(b):
        return slw[b * bc : (b + 1) * bc, :]

    for b in blocks:
        mine = slice(b * tall, (b + 1) * tall)
        for t in range(cols // wide):
            at = slice(t * wide, (t + 1) * wide)
            y = jnp.dot(proj[mine, :], tgt_ref[:, at], preferred_element_type=f32) * LOG2E
            S[mine, at] = y
            top = functools.reduce(jnp.maximum, [y[:, k : k + LANES] for k in range(0, wide, LANES)])
            M[mine, :] = top if t == 0 else jnp.maximum(M[mine, :], top)

        def first_rows(r, carry):
            m = M[r, :]
            T[r, :] = add_up([jnp.exp2(S[r, tile(t)] - m) for t in range(cc)])
            return carry

        groups(b, first_rows, 0, 4)
        for c in range(bc):
            mt, st = M[block_tile(b, c), :].T, T[block_tile(b, c), :].T
            top = jnp.max(mt, axis=0, keepdims=True)
            FS[b, c : c + 1, :] = top + jnp.log2(jnp.sum(st * jnp.exp2(mt - top), axis=0, keepdims=True))
        if b == 0:
            pl.semaphore_wait(barrier, 2 * (n_src - 1) + (n_tgt - 1))
        post_rows(0, b)

    zeros = tuple(jnp.zeros((8, LANES), f32) for t in range(cc))
    f1, peaks, sums = [], [], []
    for b in blocks:
        rows_wait(0, b).wait_recv()
        f1.append(slw_of(b) - lse([RXF[0, b, k] for k in range(n_tgt)]))
        to_columns(b, f1[b])

        def peak_cols(r, acc):
            fb = FB[r, :]
            return tuple(jnp.maximum(a, S[r, tile(t)] + fb) for t, a in enumerate(acc))

        acc = groups(b, peak_cols, tuple(jnp.full((8, LANES), -jnp.inf, f32) for t in range(cc)), 4)
        for t in range(cc):
            GS[t : t + 1, :] = jnp.max(acc[t], axis=0, keepdims=True)
        peaks.append(GS[...])
        less = [broadcast_down(SHIFT - peaks[b][t : t + 1, :]) for t in range(cc)]

        def first_cols(r, acc):
            fb = FB[r, :]
            new = []
            for t, a in enumerate(acc):
                e = jnp.exp2(S[r, tile(t)] + fb + less[t])
                S[r, tile(t)] = e
                new.append(a + e)
            return tuple(new)

        acc = groups(b, first_cols, zeros, 2)
        for t in range(cc):
            GS[t : t + 1, :] = jnp.sum(acc[t], axis=0, keepdims=True)
        sums.append(peaks[b] + (jnp.log2(GS[...]) - SHIFT))
    GS[...] = lse(sums)
    post_cols(0)
    for b in blocks:
        rows_wait(0, b).wait_send()
    cols_wait(0).wait_recv()
    g = tlw - lse([RXG[0, k] for k in range(n_src)])
    v = [jnp.exp2(peaks[b] + g) for b in blocks]

    for step in range(1, ITERS):
        last = step == ITERS - 1
        for b in blocks:
            vb = [broadcast_down(v[b][t : t + 1, :]) for t in range(cc)]

            def later_rows(r, carry):
                T[r, :] = add_up([S[r, tile(t)] * vb[t] for t in range(cc)])
                return carry

            groups(b, later_rows, 0, 4)
            for c in range(bc):
                FS[b, c : c + 1, :] = jnp.sum(T[block_tile(b, c), :].T, axis=0, keepdims=True)
            post_rows(step, b)
        cols_wait(step - 1).wait_send()
        moves, sums = [], []
        for b in blocks:
            rows_wait(step, b).wait_recv()
            moves.append(slw_of(b) - jnp.log2(sum(RXF[step, b, k] for k in range(n_tgt))))
            to_columns(b, jnp.exp2(moves[b]))

            def later_cols(r, acc):
                ub = FB[r, :]
                new = []
                for t, a in enumerate(acc):
                    e = S[r, tile(t)] * ub
                    if last:
                        S[r, tile(t)] = e
                    new.append(a + e)
                return tuple(new)

            acc = groups(b, later_cols, zeros, 4)
            for t in range(cc):
                GS[t : t + 1, :] = jnp.sum(acc[t], axis=0, keepdims=True)
            sums.append(GS[...] * v[b])
        GS[...] = sum(sums)
        post_cols(step)
        for b in blocks:
            rows_wait(step, b).wait_send()
        if last:
            peak = functools.reduce(jnp.maximum, peaks)
            ratio = [jnp.exp2(peaks[b] - peak) for b in blocks]
            for t in range(0, cc, 2):
                at = slice(t * LANES, (t + 2) * LANES)
                whole = jnp.concatenate(
                    [
                        jnp.concatenate(
                            [
                                (S[b * tall : (b + 1) * tall, tile(k)] * ratio[b][k : k + 1, :]).astype(bf16)
                                for b in blocks
                            ],
                            axis=0,
                        )
                        for k in (t, t + 1)
                    ],
                    axis=1,
                )
                W[:, at] = jnp.dot(src_ref[...], whole, preferred_element_type=f32)
        cols_wait(step).wait_recv()
        g = g + (tlw - jnp.log2(sum(RXG[step, k] for k in range(n_src))))
        if not last:
            v = [jnp.exp2(peaks[b] + g) for b in blocks]

    end = jnp.exp2(peak + g)
    total = None
    for t in range(0, cc, 4):
        at = slice(t * LANES, (t + 4) * LANES)
        x = jnp.concatenate([W[:, tile(k)] * end[k : k + 1, :] for k in range(t, t + 4)], axis=1)
        part = contract(x.astype(bf16), tgt_ref[:, at], 1, 1)
        total = part if total is None else total + part

    height = CB.shape[0]
    full, rest = dim // LANES, dim % LANES
    line = -(-dim // 8) * 8
    short = -(-rest // 8) * 8
    CB[...] = jnp.zeros(CB.shape, f32)
    for t in range(full):
        CB[t * line : t * line + dim, :] = total[:, tile(t)]
    if rest:
        plan_rows = -(-dim // LANES) * LANES
        S[0:plan_rows, 0:LANES] = jnp.zeros((plan_rows, LANES), f32)
        S[0:dim, 0:rest] = total[:, full * LANES :]
        for k in range(plan_rows // LANES):
            base = full * line + k * short
            CB[base : base + short, :] = S[tile(k), 0:LANES].T[0:short, :]

    core_id, zi, nz = lax.rem(ti, 2), lax.div(ti, 2), n_tgt // 2
    on_src = [(p, m) for p in [si] + src_peers() for m in (ti, mate[1])][1:]
    on_z = [(si, p) for p in tgt_peers()]
    over_src = [(p, ti) for p in src_peers()]
    over_z = [(si, lax.rem(zi + k, nz) * 2 + core_id) for k in range(1, nz)]

    def by_plane(d):
        return d[0] * 2 + lax.rem(d[1], 2)

    def by_column(d):
        return d[1]

    long = height * 2 // 3
    streams = [
        (0, long // (2 * n_src), 2 * n_src, on_src, by_plane, nz, over_z, zi, RX2a, RX3a),
        (long, (height - long) // n_tgt, n_tgt, on_z, by_column, n_src, over_src, si, RX2b, RX3b),
    ]

    def span(start, size):
        return pl.ds(pl.multiple_of(start, 8), size)

    def post(source, dest, send, recv, where):
        pltpu.make_async_remote_copy(
            src_ref=source, dst_ref=dest, send_sem=send, recv_sem=recv, device_id=where, device_id_type=MESH
        ).start()

    waits, old = [], [cols_wait(ITERS - 1)]
    for w, (start, size, n, peers, index, n2, peers2, me2, RXa, RXb) in enumerate(streams):
        me = index((si, ti))
        for d in peers:
            at = span(start + index(d) * size, size)
            post(CB.at[at], RXa.at[me], s2.at[w, 0], r2.at[w, 0], d)
        waits.append(whole_wait(RXa.at[pl.ds(0, n - 1)], s2.at[w, 0], r2.at[w, 0], mate))
    OUT[height : height + rc, :] = (
        jnp.concatenate([f1[b] + moves[b] for b in blocks], axis=0) + SHIFT
    ) * LN2
    OUT[height + rc : height + rc + cc, :] = g * LN2
    for wait in old:
        wait.wait_send()
    old = []
    for w, (start, size, n, peers, index, n2, peers2, me2, RXa, RXb) in enumerate(streams):
        own = CB[span(start + index((si, ti)) * size, size), :]
        waits[w].wait_recv()
        for d in peers:
            own = own + RXa[index(d)]
        RXb[me2] = own
        for d in peers2:
            post(RXb.at[me2], RXb.at[me2], s2.at[w, 1], r2.at[w, 1], d)
        old.append(waits[w])
        waits[w] = whole_wait(RXb.at[pl.ds(0, n2 - 1)], s2.at[w, 1], r2.at[w, 1], mate)
    for wait in old:
        wait.wait_send()
    old = []
    for w, (start, size, n, peers, index, n2, peers2, me2, RXa, RXb) in enumerate(streams):
        waits[w].wait_recv()
        at = span(start + index((si, ti)) * size, size)
        OUT[at, :] = sum(RXb[k] for k in range(n2))
        for d in peers:
            post(OUT.at[at], OUT.at[at], s2.at[w, 2], r2.at[w, 2], d)
        old.append(waits[w])
        waits[w] = whole_wait(OUT.at[pl.ds(0, (n - 1) * size)], s2.at[w, 2], r2.at[w, 2], mate)
    for wait in old:
        wait.wait_send()
    for wait in waits:
        wait.wait()


def unpack(scale, dim, height, lines, f_out, g_out, core_out):
    rc, cc = f_out.shape[0], g_out.shape[0]
    f_out[...] = lines[height : height + rc, :]
    g_out[...] = lines[height + rc : height + rc + cc, :]
    full, rest = dim // LANES, dim % LANES
    line = -(-dim // 8) * 8
    short = -(-rest // 8) * 8
    for t in range(full):
        core_out[:, tile(t)] = lines[t * line : t * line + dim, :] * scale
    if rest:
        for k in range(-(-dim // LANES)):
            base = full * line + k * short
            block = jnp.concatenate(
                [lines[base : base + short, :], jnp.zeros((LANES - short, LANES), jnp.float32)], axis=0
            ).T * scale
            count = min(LANES, dim - k * LANES)
            core_out[k * LANES : k * LANES + count, full * LANES :] = block[0:count, 0:rest]


def per_device(n_src, n_tgt, src_emb_t, tgt_emb_t, core, src_logw, tgt_logw):
    dim, rows = src_emb_t.shape
    cols = tgt_emb_t.shape[1]
    f32 = jnp.float32
    line, short = -(-dim // 8) * 8, -(-(dim % LANES) // 8) * 8
    need = (dim // LANES) * line + -(-dim // LANES) * short
    nz = n_tgt // 2
    unit = 16 * math.lcm(n_src, nz)
    height = -(-need // (3 * unit)) * 3 * unit
    long = height * 2 // 3
    block, brief = long // (2 * n_src), (height - long) // n_tgt
    sems = pltpu.SemaphoreType.DMA
    vmem = pl.BlockSpec(memory_space=pltpu.VMEM)
    rc, cc = rows // LANES, cols // LANES
    hbm = pl.BlockSpec(memory_space=pltpu.HBM)
    lines = pl.pallas_call(
        functools.partial(kernel, n_src, n_tgt),
        out_shape=jax.ShapeDtypeStruct((height + rc + cc, LANES), f32),
        in_specs=[hbm] * 5,
        out_specs=vmem,
        scratch_shapes=[
            pltpu.VMEM(src_emb_t.shape, jnp.bfloat16),
            pltpu.VMEM(tgt_emb_t.shape, jnp.bfloat16),
            pltpu.VMEM(core.shape, f32),
            pltpu.VMEM((rc, LANES), f32),
            pltpu.VMEM((cc, LANES), f32),
            sems((5,)),
            pltpu.VMEM((rows, cols), f32),
            pltpu.VMEM((rows, dim), jnp.bfloat16),
            pltpu.VMEM((rows, LANES), f32),
            pltpu.VMEM((rows, LANES), f32),
            pltpu.VMEM((rows, LANES), f32),
            pltpu.VMEM((BLOCKS, rc // BLOCKS, LANES), f32),
            pltpu.VMEM((cc, LANES), f32),
            pltpu.VMEM((ITERS, BLOCKS, n_tgt, rc // BLOCKS, LANES), f32),
            pltpu.VMEM((ITERS, n_src, cc, LANES), f32),
            pltpu.VMEM((dim, cols), f32),
            pltpu.VMEM((height, LANES), f32),
            pltpu.VMEM((2 * n_src, block, LANES), f32),
            pltpu.VMEM((nz, block, LANES), f32),
            pltpu.VMEM((n_tgt, brief, LANES), f32),
            pltpu.VMEM((n_src, brief, LANES), f32),
            sems((ITERS, BLOCKS)), sems((ITERS, BLOCKS)),
            sems((ITERS,)), sems((ITERS,)),
            sems((2, 3)), sems((2, 3)),
        ],
        compiler_params=pltpu.CompilerParams(
            collective_id=0, has_side_effects=True, vmem_limit_bytes=64 * 1024 * 1024
        ),
    )(src_emb_t, tgt_emb_t, core, src_logw.reshape(rc, LANES), tgt_logw.reshape(cc, LANES))
    f, g, new = pl.pallas_call(
        functools.partial(unpack, dim / (rows * n_src), dim, height),
        out_shape=(
            jax.ShapeDtypeStruct((rc, LANES), f32),
            jax.ShapeDtypeStruct((cc, LANES), f32),
            jax.ShapeDtypeStruct((dim, dim), f32),
        ),
        in_specs=[vmem],
        out_specs=(vmem,) * 3,
        compiler_params=pltpu.CompilerParams(vmem_limit_bytes=64 * 1024 * 1024),
    )(lines)
    return f.reshape(rows), g.reshape(cols), new


def solution(mesh):
    placed = (P(None, "src"), P(None, "tgt"), P(), P("src"), P("tgt"))
    body = functools.partial(per_device, mesh.shape["src"], mesh.shape["tgt"])
    return jax.shard_map(
        body, mesh=mesh, in_specs=placed, out_specs=(P("src"), P("tgt"), P()), check_vma=False
    )
```
